32 devices in a mesh: groups: 2 (over x), row: 16 (over z, y, core).
Axes of the slice: x: 2, y: 2, z: 4, core: 2. Of those that a mesh axis runs over, the one named last changes fastest.
Arguments:
- inputs: bfloat16 [1024, 8192], P(('groups', 'row')), parts along dimension 0, may hold values from -6 to 6
- input_factor: bfloat16 [16384, 8192], P(('groups', 'row')), parts along dimension 0, as said below
- out_grads: bfloat16 [1024, 16384], P(('groups', 'row')), parts along dimension 0, may hold values from -6 to 6
- output_factor: float32 [32768, 4096], P(('groups', 'row')), parts along dimension 0, may hold values from -6 to 6
Outputs:
- updated_factor: float32 [32768, 4096], P(('groups', 'row')), parts along dimension 0
The draws below stay inside these ranges and needn't reach their ends.
There are 2 independent parts, one for each index of `groups`. The reference program is written for one: setup_inputs(seed, part) draws one part's arguments, and reference() takes and returns one part's arrays. A program takes and returns all parts, laid end to end along the dimension named above; each array names one. Nothing has to cross between parts.
Inputs may be any that keep to these rules, and one draw needn't show every extreme that they name: input_factor is symmetric.
All inputs are finite; a program needn't handle non-finite values.
Results may differ from the reference program's by a relative error of at most 0.0041.
Values may be sent and summed in bfloat16 or wider, within the bound.
No kernel may reach another device: no remote copies, remote signals or barrier semaphores. Data moves between devices by JAX's collectives and lax.ppermute only.
A program may use at most 192 MiB of HBM per device.

```python
import jax
import jax.numpy as jnp

DIN = 8192
DOUT = 16384
SLAB = 4096
TOKENS = 512
N_ROW = 16


def draw_input_factor(key, part):
    base = jax.random.truncated_normal(key, -4.0, 4.0, (DIN, DIN), jnp.float32)
    symmetric = (base + base.T) * 0.5 ** 0.5
    width = DIN // N_ROW
    row_block = jnp.arange(DIN, dtype=jnp.int32) // width
    same_block = (row_block[:, None] == row_block[None, :]).astype(jnp.float32)
    boosted = symmetric * (1.0 + 2.0 * same_block)
    return (boosted * float(DIN) ** (-0.5)).astype(jnp.bfloat16)


def block_scale(key, shape, split, low, high):
    def one(position, parts):
        draws = jax.random.uniform(jax.random.fold_in(jax.random.fold_in(key, 6), position), (parts,), jnp.float32, low / len(split), high / len(split))
        return jnp.repeat(jnp.exp(draws), shape[position] // parts).reshape((-1,) + (1,) * (len(shape) - position - 1))

    factor_of = one(*split[0])
    for cut in split[1:]:
        factor_of = factor_of * one(*cut)
    return factor_of


def scatter_about(rng, dims, scale, reach, cuts=(), kind=jnp.bfloat16):
    level = block_scale(rng, dims, cuts, -0.22, 0.18) if cuts else 1.0
    values = jax.random.normal(rng, dims, jnp.float32) * scale * level
    return jnp.minimum(jnp.maximum(values, -reach), reach).astype(kind)


def setup_inputs(seed: int = 0, part: int = 0) -> dict:
    splits = jax.random.split(jax.random.key(seed), 5)
    own_keys = jax.random.split(jax.random.fold_in(splits[4], part), 5)
    return {
        "inputs": scatter_about(own_keys[0], (TOKENS, DIN), 1.0, 6.0, ((0, 16),)),
        "input_factor": draw_input_factor(jax.random.fold_in(jax.random.fold_in(splits[4], part), 71), part),
        "out_grads": scatter_about(own_keys[2], (TOKENS, DOUT), 1.0, 6.0, ((0, 16),)),
        "output_factor": scatter_about(own_keys[3], (DOUT, SLAB), 1.0, 6.0, ((0, 16),), jnp.float32),
    }


def reference(inputs, input_factor, out_grads, output_factor):
    projected = jnp.dot(inputs, input_factor, preferred_element_type=jnp.float32).astype(jnp.bfloat16)
    summed = jnp.dot(projected, inputs.T, preferred_element_type=jnp.float32)
    gram = (summed * (float(DIN) ** -0.5)).astype(jnp.bfloat16)
    left = jnp.dot(out_grads.T, gram, preferred_element_type=jnp.float32).astype(jnp.bfloat16)
    update = jnp.dot(left, out_grads[:, :SLAB], preferred_element_type=jnp.float32)
    return output_factor + update * (1.0 / TOKENS)
```

```python
import functools

import jax
import jax.numpy as jnp
from jax import lax
from jax.experimental import pallas as pl
from jax.experimental.pallas import tpu as pltpu
from jax.sharding import PartitionSpec as P

BF16 = jnp.bfloat16
F32 = jnp.float32
VMEM_LIMIT = 56 * 1024 * 1024


def permute(value, perm):
    return lax.ppermute(value, "row", perm)


def core_perm(n):
    return [(i, i ^ 1) for i in range(n)]


def y_perm(n):
    return [(i, i ^ 2) for i in range(n)]


def plane_perm(n, step):
    return [(i, (i + 4 * step) % n) for i in range(n)]


def takes_extra(plane, planes):
    return (plane % 2 == 0) == (plane < planes // 2)


def spread(value):
    n = lax.axis_size("row")
    two = jnp.concatenate([value, permute(value, y_perm(n))], 0)
    return two, permute(two, core_perm(n))


def block_row(i, place, planes):
    step, inner = i // 4, i % 4
    plane = lax.rem(place // 4 + planes - step, planes)
    y = lax.rem(place // 2, 2)
    core = lax.rem(place, 2)
    y = 1 - y if inner % 2 else y
    core = 1 - core if inner >= 2 else core
    return plane * 4 + y * 2 + core


def gram_kernel(place_ref, *refs, planes, chunk, width, scale):
    pieces, a_ref, out_ref, acc, whole = refs[: 2 * planes], refs[-4], refs[-3], refs[-2], refs[-1]
    j = pl.program_id(0)
    place = place_ref[0]
    shard = pieces[0].shape[0] // 2

    @pl.when(j == 0)
    def _():
        acc[...] = jnp.zeros_like(acc)

    tokens = jnp.concatenate([p[:, pl.ds(pl.multiple_of(j * chunk, chunk), chunk)] for p in pieces], 0)
    part = lax.dot_general(tokens, a_ref[...], (((1,), (1,)), ((), ())), preferred_element_type=F32)
    acc[...] += part * jnp.where(j < width // chunk, 0.5, 1.0)

    @pl.when(j == pl.num_programs(0) - 1)
    def _():
        own = a_ref.shape[0]
        left = pl.multiple_of(lax.rem(place, 4) * own, own)
        total = acc.shape[0]
        for i in range(4 * planes):
            row = pl.multiple_of(block_row(i, place, planes) * shard, shard)
            whole[0, pl.ds(row, shard), :] = acc[i * shard:(i + 1) * shard, :].astype(BF16)
            piece = pieces[i // 2]
            whole[1, pl.ds(row, shard), :] = piece[(i % 2) * shard:(i % 2 + 1) * shard, pl.ds(left, own)]
        half = lax.dot_general(whole[1], whole[0], (((1,), (1,)), ((), ())), preferred_element_type=F32)
        out_ref[...] = (half + half.T) * scale


def gram_part(pieces, input_factor, place, planes):
    own, features = input_factor.shape
    width = features // planes
    chunk = min(1024, width)
    steps = (planes // 2 + 1) * width // chunk
    tokens = sum(p.shape[0] for p in pieces)
    per_plane = width // chunk
    columns = features // chunk

    def a_map(j, place_ref):
        return 0, lax.rem(place_ref[0] // 4 * per_plane + j, columns)

    return pl.pallas_call(
        functools.partial(gram_kernel, planes=planes, chunk=chunk, width=width, scale=float(features) ** -0.5),
        grid_spec=pltpu.PrefetchScalarGridSpec(
            num_scalar_prefetch=1,
            grid=(steps,),
            in_specs=[pl.BlockSpec(memory_space=pltpu.VMEM)] * len(pieces) + [pl.BlockSpec((own, chunk), a_map)],
            out_specs=pl.BlockSpec((tokens, tokens), lambda j, _: (0, 0)),
            scratch_shapes=[pltpu.VMEM((tokens, own), F32), pltpu.VMEM((2, tokens, own), BF16)],
        ),
        out_shape=jax.ShapeDtypeStruct((tokens, tokens), F32),
        compiler_params=pltpu.CompilerParams(vmem_limit_bytes=VMEM_LIMIT),
        cost_estimate=pl.CostEstimate(
            flops=2 * tokens * own * (steps * chunk + tokens), bytes_accessed=2 * own * steps * chunk, transcendentals=0
        ),
    )(place, *pieces, input_factor)


def update_kernel(place_ref, *refs, planes, scale):
    pieces = refs[: 2 * planes]
    gram_ref, grads_ref, factor_ref, out_ref, left_abs, left = refs[2 * planes:]
    place = place_ref[0]
    shard = pieces[0].shape[0] // 2

    @pl.when(pl.program_id(0) == 0)
    def _():
        left_abs[...] = jnp.dot(gram_ref[...], grads_ref[...], preferred_element_type=F32).astype(BF16)
        rows = []
        for i in range(4 * planes):
            row = pl.multiple_of(block_row(i, place, planes) * shard, shard)
            rows.append(left_abs[pl.ds(row, shard), :])
        left[...] = jnp.concatenate(rows, 0).T

    slab = jnp.concatenate([p[...] for p in pieces], 0)
    out_ref[...] = factor_ref[...] + jnp.dot(left[...], slab, preferred_element_type=F32) * scale


def update(pieces, gram, grads, output_factor, place, planes):
    rows, columns = output_factor.shape
    tokens = gram.shape[0]
    chunk = min(512, columns)
    shard2 = pieces[0].shape[0]
    return pl.pallas_call(
        functools.partial(update_kernel, planes=planes, scale=1.0 / tokens),
        grid_spec=pltpu.PrefetchScalarGridSpec(
            num_scalar_prefetch=1,
            grid=(columns // chunk,),
            in_specs=[pl.BlockSpec((shard2, chunk), lambda j, _: (0, j))] * len(pieces)
            + [
                pl.BlockSpec((tokens, tokens), lambda j, _: (0, 0)),
                pl.BlockSpec((tokens, rows), lambda j, _: (0, 0)),
                pl.BlockSpec((rows, chunk), lambda j, _: (0, j)),
            ],
            out_specs=pl.BlockSpec((rows, chunk), lambda j, _: (0, j)),
            scratch_shapes=[pltpu.VMEM((tokens, rows), BF16), pltpu.VMEM((rows, tokens), BF16)],
        ),
        out_shape=jax.ShapeDtypeStruct((rows, columns), F32),
        compiler_params=pltpu.CompilerParams(vmem_limit_bytes=VMEM_LIMIT),
        cost_estimate=pl.CostEstimate(
            flops=2 * rows * tokens * (columns + tokens), bytes_accessed=8 * rows * columns, transcendentals=0
        ),
    )(place, *pieces, gram, grads, output_factor)


def sum_over_row(part, place):
    n = lax.axis_size("row")
    core, y = place % 2, place // 2 % 2

    def split(value, which):
        halves = value.reshape(2, value.shape[0] // 2, value.shape[1])
        pick = functools.partial(lax.dynamic_index_in_dim, halves, axis=0, keepdims=False)
        return pick(which), pick(1 - which)

    def join(mine, other, which):
        return jnp.where(which == 0, jnp.concatenate([mine, other], 0), jnp.concatenate([other, mine], 0))

    mine, other = split(part, core)
    mine = mine + permute(other, core_perm(n))
    mine, other = split(mine, y)
    mine = mine + permute(other.astype(BF16), y_perm(n)).astype(F32)
    step = 4
    while step < n:
        mine = mine + permute(mine.astype(BF16), [(i, i ^ step) for i in range(n)]).astype(F32)
        step *= 2
    mine = mine.astype(BF16)
    mine = join(mine, permute(mine, y_perm(n)), y)
    return join(mine, permute(mine, core_perm(n)), core)


def per_device(inputs, input_factor, out_grads, output_factor):
    n = lax.axis_size("row")
    planes = n // 4
    place = lax.axis_index("row")
    plane = place // 4
    half = planes // 2
    width = inputs.shape[1] // planes

    turned = lax.dynamic_slice_in_dim(jnp.concatenate([inputs, inputs], 1), plane * width, inputs.shape[1], 1)
    turned = jnp.concatenate([turned, turned[:, : (half + 1) * width]], 1)

    def main(step):
        return turned[:, step * width:(step + half) * width]

    def extra(step):
        return turned[:, (step + half) * width:(step + half + 1) * width]

    wanted = [takes_extra(q, planes) for q in range(planes)]
    steps = sorted(range(1, planes), key=lambda k: -min(k, planes - k))
    arrived = {}
    for k in steps:
        some = [(i, j) for i, j in plane_perm(n, k) if wanted[j // 4]]
        arrived[k] = (permute(main(k), plane_perm(n, k)), permute(extra(k), some))
    mine = jnp.asarray(wanted)[plane]
    arrived[0] = (main(0), jnp.where(mine, extra(0), jnp.zeros_like(extra(0))))
    pieces = []
    for k in range(planes):
        pieces += spread(jnp.concatenate(arrived[k], 1))

    slab_width = output_factor.shape[1]
    hold, _ = lax.optimization_barrier((out_grads, arrived[half][0]))
    grad_cols = lax.all_to_all(hold, "row", split_axis=1, concat_axis=0, tiled=True)
    slab = hold[:, :slab_width]
    slab_pieces = []
    for k in range(planes):
        slab_pieces += spread(permute(slab, plane_perm(n, k)) if k else slab)

    scalar = place.reshape(1)
    gram = sum_over_row(gram_part(pieces, input_factor, scalar, planes), place)
    return update(slab_pieces, gram, grad_cols, output_factor, scalar, planes)


def solution(mesh):
    spec = P(("groups", "row"), None)
    return jax.shard_map(per_device, mesh=mesh, in_specs=(spec,) * 4, out_specs=spec, check_vma=False)
```

```python
import functools

import jax
import jax.numpy as jnp
from jax import lax
from jax.experimental import pallas as pl
from jax.experimental.pallas import tpu as pltpu
from jax.sharding import PartitionSpec as P

BF16 = jnp.bfloat16
F32 = jnp.float32
MIB = 1024 * 1024


def permute(value, perm):
    return lax.ppermute(value, "row", perm)


def core_perm(n):
    return [(i, i ^ 1) for i in range(n)]


def y_perm(n):
    return [(i, i ^ 2) for i in range(n)]


def plane_perm(n, step):
    return [(i, (i + 4 * step) % n) for i in range(n)]


def call(body, place, inputs, outputs, scratch=(), limit=8 * MIB, flops=0, bytes_accessed=0, far=()):
    vmem = pl.BlockSpec(memory_space=pltpu.VMEM)
    anywhere = pl.BlockSpec(memory_space=pltpu.HBM)
    return pl.pallas_call(
        body,
        in_specs=[pl.BlockSpec(memory_space=pltpu.SMEM)]
        + [anywhere if i in far else vmem for i in range(len(inputs))],
        out_specs=[vmem] * len(outputs),
        out_shape=[jax.ShapeDtypeStruct(shape, dtype) for shape, dtype in outputs],
        scratch_shapes=list(scratch),
        compiler_params=pltpu.CompilerParams(vmem_limit_bytes=limit),
        cost_estimate=pl.CostEstimate(flops=flops, bytes_accessed=bytes_accessed, transcendentals=0),
    )(place, *inputs)


def pack(place, inputs, wanted):
    outputs = [
        ((sum(inputs[i].shape[0] for i in each), inputs[each[0]].shape[1]), inputs[each[0]].dtype) for each in wanted
    ]

    def body(place_ref, *refs):
        del place_ref
        ins, outs = refs[: len(inputs)], refs[len(inputs):]
        for each, out in zip(wanted, outs):
            row = 0
            for i in each:
                out[row:row + ins[i].shape[0], :] = ins[i][...]
                row += ins[i].shape[0]

    return call(body, place, inputs, outputs)


def token_blocks(groups):
    return [(k, y, core) for group in groups for core in (0, 1) for y in (0, 1) for k in group]


def shard_of(place, block, planes):
    back, other_y, other_core = block
    plane = lax.rem(place // 4 + planes - back, planes)
    y, core = lax.rem(place // 2, 2), lax.rem(place, 2)
    return plane * 4 + (1 - y if other_y else y) * 2 + (1 - core if other_core else core)


def messages(inputs, place, planes):
    rows, features = inputs.shape
    width = features // planes
    used = planes // 2 + 1

    def body(place_ref, x_ref, *outs):
        plane = place_ref[0] // 4
        for k, out in enumerate(outs):
            for j in range(used):
                left = pl.multiple_of(lax.rem(plane + k + j, planes) * width, width)
                out[:, j * width:(j + 1) * width] = x_ref[:, pl.ds(left, width)]

    return call(body, place, [inputs], [((rows, used * width), inputs.dtype)] * planes)


def gram_part(pieces, groups, input_factor, place, planes):
    own, features = input_factor.shape
    width = features // planes
    used = planes // 2 + 1
    blocks = token_blocks(groups)
    tokens = sum(p.shape[0] for p in pieces)
    shard = tokens // len(blocks)
    count = len(pieces)
    scale = float(features) ** -0.5

    def body(place_ref, *refs):
        ins, a_ref, mine_ref, other_ref, near, whole, total, sems = (
            refs[:count], refs[count], *refs[count + 1:]
        )
        here = place_ref[0]
        copies = []
        for j in range(used):
            left = pl.multiple_of(lax.rem(here // 4 + j, planes) * width, width)
            copies.append(pltpu.make_async_copy(a_ref.at[:, pl.ds(left, width)], near.at[j], sems.at[j]))
            copies[-1].start()
        acc = None
        for j in range(used):
            copies[j].wait()
            rows = jnp.concatenate([p[:, j * width:(j + 1) * width] for p in ins], 0)
            part = lax.dot_general(rows, near[j], (((1,), (1,)), ((), ())), preferred_element_type=F32)
            part = part * 0.5 if j in (0, planes // 2) else part
            acc = part if acc is None else acc + part
        left = pl.multiple_of(lax.rem(here, 4) * own, own)
        at = 0
        for piece in ins:
            for low in range(0, piece.shape[0], shard):
                row = pl.multiple_of(shard_of(here, blocks[at // shard], planes) * shard, shard)
                mine = acc[at:at + shard, :]
                high = mine.astype(BF16)
                whole[0, pl.ds(row, shard), :] = high
                whole[1, pl.ds(row, shard), :] = (mine - high.astype(F32)).astype(BF16)
                whole[2, pl.ds(row, shard), :] = piece[low:low + shard, pl.ds(left, own)]
                at += shard
        half = lax.dot_general(whole[2], whole[0], (((1,), (1,)), ((), ())), preferred_element_type=F32)
        half += lax.dot_general(whole[2], whole[1], (((1,), (1,)), ((), ())), preferred_element_type=F32)
        total[...] = (half + half.T) * scale
        core = lax.rem(here, 2)
        mine_ref[...] = total[pl.ds(pl.multiple_of(core * (tokens // 2), tokens // 2), tokens // 2), :]
        other_ref[...] = total[pl.ds(pl.multiple_of((1 - core) * (tokens // 2), tokens // 2), tokens // 2), :]

    return call(
        body, place, [*pieces, input_factor], [((tokens // 2, tokens), F32)] * 2,
        scratch=[
            pltpu.VMEM((used, own, width), BF16), pltpu.VMEM((3, tokens, own), BF16), pltpu.VMEM((tokens, tokens), F32),
            pltpu.SemaphoreType.DMA((used,)),
        ],
        limit=46 * MIB, far=(count,), flops=2 * tokens * own * (used * width + tokens),
        bytes_accessed=2 * own * used * width,
    )


def add_split(mine, other, place, bit, earlier):
    rows, columns = mine.shape
    half = rows // 2

    def body(place_ref, mine_ref, other_ref, *refs):
        keep_ref, give_ref, total = refs[-3:]
        which = lax.rem(place_ref[0] // bit, 2)
        total[...] = mine_ref[...] + other_ref[...].astype(F32)
        keep_ref[...] = total[pl.ds(pl.multiple_of(which * half, half), half), :]
        give_ref[...] = total[pl.ds(pl.multiple_of((1 - which) * half, half), half), :].astype(BF16)

    return call(
        body, place, [mine, other, *earlier], [((half, columns), F32), ((half, columns), BF16)],
        scratch=[pltpu.VMEM((rows, columns), F32)], far=tuple(range(2, 2 + len(earlier))),
    )


def add(mine, other, place, earlier=()):
    def body(place_ref, mine_ref, other_ref, *refs):
        del place_ref
        sum_ref, low_ref = refs[-2:]
        total = mine_ref[...] + other_ref[...].astype(F32)
        sum_ref[...] = total
        low_ref[...] = total.astype(BF16)

    return call(
        body, place, [mine, other, *earlier], [(mine.shape, F32), (mine.shape, BF16)],
        far=tuple(range(2, 2 + len(earlier))),
    )


def join(mine, other, place, bit):
    rows, columns = mine.shape

    def body(place_ref, mine_ref, other_ref, out_ref):
        which = lax.rem(place_ref[0] // bit, 2)
        out_ref[pl.ds(pl.multiple_of(which * rows, rows), rows), :] = mine_ref[...]
        out_ref[pl.ds(pl.multiple_of((1 - which) * rows, rows), rows), :] = other_ref[...]

    return call(body, place, [mine, other], [((2 * rows, columns), mine.dtype)])[0]


def update(slab, blocks, halves, grads, output_factor, place, planes):
    rows, columns = output_factor.shape
    tokens = grads.shape[0]
    shard = tokens // len(blocks)
    chunk = min(1024, columns)
    scale = 1.0 / tokens
    half = tokens // 2

    def body(place_ref, *refs):
        slabs = refs[: len(slab)]
        mine_ref, other_ref, grads_ref, factor_ref, out_ref, gram, left_abs, left = refs[len(slab):]
        here = place_ref[0]

        @pl.when(pl.program_id(0) == 0)
        def _():
            core = lax.rem(here, 2)
            gram[pl.ds(pl.multiple_of(core * half, half), half), :] = mine_ref[...]
            gram[pl.ds(pl.multiple_of((1 - core) * half, half), half), :] = other_ref[...]
            left_abs[...] = jnp.dot(gram[...], grads_ref[...], preferred_element_type=F32).astype(BF16)
            order = []
            for block in blocks:
                row = pl.multiple_of(shard_of(here, block, planes) * shard, shard)
                order.append(left_abs[pl.ds(row, shard), :])
            left[...] = jnp.concatenate(order, 0).T

        part = jnp.concatenate([s[...] for s in slabs], 0)
        out_ref[...] = factor_ref[...] + jnp.dot(left[...], part, preferred_element_type=F32) * scale

    vmem = pl.BlockSpec(memory_space=pltpu.VMEM)
    return pl.pallas_call(
        body,
        grid=(columns // chunk,),
        in_specs=[pl.BlockSpec(memory_space=pltpu.SMEM)]
        + [pl.BlockSpec((s.shape[0], chunk), lambda j: (0, j)) for s in slab]
        + [vmem, vmem, vmem, pl.BlockSpec((rows, chunk), lambda j: (0, j))],
        out_specs=pl.BlockSpec((rows, chunk), lambda j: (0, j)),
        scratch_shapes=[
            pltpu.VMEM((tokens, tokens), BF16), pltpu.VMEM((tokens, rows), BF16), pltpu.VMEM((rows, tokens), BF16)
        ],
        out_shape=jax.ShapeDtypeStruct((rows, columns), F32),
        compiler_params=pltpu.CompilerParams(vmem_limit_bytes=48 * MIB),
        cost_estimate=pl.CostEstimate(
            flops=2 * rows * tokens * (columns + tokens), bytes_accessed=8 * rows * columns, transcendentals=0
        ),
    )(place, *slab, *halves, grads, output_factor)


def by_owner(grads, place, earlier, n):
    rows, columns = grads.shape
    width = columns // n

    def body(place_ref, grads_ref, *refs):
        del place_ref
        out = refs[-1]
        for i in range(n):
            out[i * rows:(i + 1) * rows, :] = grads_ref[:, i * width:(i + 1) * width]

    return call(
        body, place, [grads, *earlier], [((n * rows, width), grads.dtype)], far=tuple(range(1, 1 + len(earlier)))
    )[0]


def per_device(inputs, input_factor, out_grads, output_factor):
    n = lax.axis_size("row")
    planes = n // 4
    half = planes // 2
    place = lax.axis_index("row").reshape(1)
    near = sorted((k for k in range(1, planes) if k != half), key=lambda k: min(k, planes - k))
    groups = [[0], near, [half]]
    slab = out_grads[:, : output_factor.shape[1]]

    def across(value):
        return permute(value, y_perm(n))

    def other_core(value):
        return permute(value, core_perm(n))

    def ahead(value, k):
        return permute(value, plane_perm(n, k))

    send = messages(inputs, place, planes)
    got = {k: ahead(send[k], k) for k in near}
    crossed_0, slab_crossed_0 = across(send[0]), across(slab)

    first = [got[k] for k in near]
    count = len(near)
    near_send, far_send, pair_0 = pack(
        place, [*first, send[half], send[0], crossed_0, slab_crossed_0],
        [list(range(count)), [count], [count + 1, count + 2]],
    )
    got[half] = ahead(far_send, half)
    crossed_near = across(near_send)
    pair_0_other = other_core(pair_0)

    far_cross, pair_near, slab_send = pack(
        place, [got[half], near_send, crossed_near, slab, pair_0_other], [[0], [1, 2], [3]]
    )
    crossed_far = across(far_cross)
    pair_near_other = other_core(pair_near)
    slab_got = [ahead(slab_send, k) for k in near]

    pair_far, slab_near, slab_far_send = pack(
        place, [far_cross, crossed_far, *slab_got, slab_send, pair_near_other],
        [[0, 1], list(range(2, 2 + count)), [2 + count]],
    )
    pair_far_other = other_core(pair_far)
    slab_far = ahead(slab_far_send, half)
    slab_crossed_near = across(slab_near)
    grads = by_owner(out_grads, place, [far_cross], n)
    own_grads = lax.all_to_all(grads, "row", split_axis=0, concat_axis=0, tiled=True)

    pieces = [pair_0, pair_0_other, pair_near, pair_near_other, pair_far, pair_far_other]
    mine, other = gram_part(pieces, groups, input_factor, place, planes)

    mine, other = add_split(mine, other_core(other), place, 2, [])
    slab_crossed_far = across(slab_far)
    mine, low = add(mine, across(other), place)
    step = 4
    while step < n:
        mine, low = add(mine, permute(low, [(i, i ^ step) for i in range(n)]), place)
        step *= 2
    *slabs, low = pack(
        place, [slab, slab_crossed_0, slab_near, slab_crossed_near, slab_far, slab_crossed_far, low],
        [[0, 1], [2, 3], [4, 5], [6]],
    )
    slabs = sum(([s, other_core(s)] for s in slabs), [])
    low = join(low, across(low), place, 2)
    return update(
        slabs, token_blocks(groups), [low, other_core(low)], own_grads, output_factor, place, planes
    )


def solution(mesh):
    spec = P(("groups", "row"), None)
    return jax.shard_map(per_device, mesh=mesh, in_specs=(spec,) * 4, out_specs=spec, check_vma=False)
```

```python
import enum

import jax
import jax.numpy as jnp
from jax import lax
from jax.experimental import pallas as pl
from jax.experimental.pallas import tpu as pltpu
from jax.sharding import PartitionSpec as P

BF16 = jnp.bfloat16
F32 = jnp.float32
MIB = 1024 * 1024
GRAM_ROWS_VMEM = 44 * MIB
UPDATE_VMEM = 22 * MIB
FETCH = True


class N(enum.Enum):
    near = enum.auto()
    rows = enum.auto()
    factor = enum.auto()
    mine = enum.auto()
    other = enum.auto()
    far = enum.auto()
    out = enum.auto()
    earlier = enum.auto()
    own = enum.auto()
    give = enum.auto()
    x = enum.auto()
    cross = enum.auto()
    grads = enum.auto()
    slab = enum.auto()
    chip = enum.auto()
    pair = enum.auto()
    crossed = enum.auto()
    sent = enum.auto()
    grads_crossed = enum.auto()
    slab_cross = enum.auto()
    send = enum.auto()
    between = enum.auto()
    products = enum.auto()
    late = enum.auto()
    keep = enum.auto()
    low = enum.auto()
    sum = enum.auto()
    grads_cross = enum.auto()
    far_slab = enum.auto()
    early = enum.auto()
    gram = enum.auto()
    slabs = enum.auto()


def permute(value, perm):
    return lax.ppermute(value, "row", perm)


def core_perm(n):
    return [(i, i ^ 1) for i in range(n)]


def y_perm(n):
    return [(i, i ^ 2) for i in range(n)]


def plane_perm(n, step):
    return [(i, (i + 4 * step) % n) for i in range(n)]


def call(body, place, inputs, outputs, scratch=(), limit=4 * MIB, flops=0, bytes_accessed=0, far=()):
    vmem = pl.BlockSpec(memory_space=pltpu.VMEM)
    anywhere = pl.BlockSpec(memory_space=pltpu.HBM)
    names = [*inputs, *outputs]

    def kernel(place_ref, *refs):
        body(place_ref[0], dict(zip(names, refs)), *refs[len(names):])

    results = pl.pallas_call(
        kernel,
        in_specs=[pl.BlockSpec(memory_space=pltpu.SMEM)] + [anywhere if k in far else vmem for k in inputs],
        out_specs=[vmem] * len(outputs),
        out_shape=[jax.ShapeDtypeStruct(shape, dtype) for shape, dtype in outputs.values()],
        scratch_shapes=list(scratch),
        compiler_params=pltpu.CompilerParams(vmem_limit_bytes=limit),
        cost_estimate=pl.CostEstimate(flops=flops, bytes_accessed=bytes_accessed, transcendentals=0),
    )(place, *inputs.values())
    return dict(zip(outputs, results))


def stack(out, refs):
    row = 0
    for ref in refs:
        out[row:row + ref.shape[0], :] = ref[...]
        row += ref.shape[0]


def token_blocks(groups):
    return [(k, y, core) for group in groups for core in (0, 1) for y in (0, 1) for k in group]


def shard_of(place, block, planes):
    back, other_y, other_core = block
    plane = lax.rem(place // 4 + planes - back, planes)
    y, core = lax.rem(place // 2, 2), lax.rem(place, 2)
    return plane * 4 + (1 - y if other_y else y) * 2 + (1 - core if other_core else core)


def half_block(place, planes, other):
    y = lax.rem(place // 2, 2)
    y = 1 - y if other else y
    return jnp.where(place // 4 < planes // 2, y, 1 - y)


def gram_rows(pieces, input_factor, place, planes):
    own, features = input_factor.shape
    width = features // planes
    half = planes // 2
    columns = pieces[0].shape[1]
    tokens = sum(p.shape[0] for p in pieces)
    count = len(pieces)

    def body(here, refs, sems):
        near, acc = refs[N.near], refs[N.rows]
        copies = []
        for j in range(half + 1):
            left = lax.rem(here // 4 + j, planes) * width
            size = width
            if j == half:
                size = width // 2
                left = left + half_block(here, planes, False) * size
            copies.append(
                pltpu.make_async_copy(
                    refs[N.factor].at[:, pl.ds(pl.multiple_of(left, size), size)],
                    near.at[:, j * width:j * width + size], sems.at[j],
                )
            )
            copies[-1].start()
        for j, copy in enumerate(copies):
            copy.wait()
            at = slice(j * width, min((j + 1) * width, columns))
            rows = jnp.concatenate([refs[i][:, at] for i in range(count)], 0)
            part = lax.dot_general(rows, near[:, at], (((1,), (1,)), ((), ())), preferred_element_type=F32)
            acc[...] = part * 0.5 if j == 0 else acc[...] + part

    out = call(
        body, place, {**dict(enumerate(pieces)), N.factor: input_factor},
        {N.rows: ((tokens, own), F32), N.near: ((own, columns), input_factor.dtype)},
        scratch=[pltpu.SemaphoreType.DMA((half + 1,))], limit=GRAM_ROWS_VMEM, far=(N.factor,),
        flops=2 * tokens * own * columns, bytes_accessed=2 * own * columns,
    )
    return out[N.rows], out[N.near]


def gram_part(rows, near, before, after, groups, place, planes, features, earlier):
    own, columns = near.shape
    width = features // planes
    blocks = token_blocks(groups)
    pieces = [*before, *after]
    tokens = sum(p.shape[0] for p in pieces)
    shard = tokens // len(blocks)
    count = len(pieces)
    scale = float(features) ** -0.5

    def body(here, refs, whole, total):
        ins = [refs[i] for i in range(count)]
        last = jnp.concatenate([refs[i][...] for i in range(len(before), count)], 0)
        near = refs[N.near]
        acc = 0.5 * lax.dot_general(
            last[:, :width], near[:, :width], (((1,), (1,)), ((), ())), preferred_element_type=F32
        )
        acc += lax.dot_general(last[:, width:], near[:, width:], (((1,), (1,)), ((), ())), preferred_element_type=F32)
        left = pl.multiple_of(lax.rem(here, 4) * own, own)
        at, first = 0, refs[N.rows].shape[0]
        for piece in ins:
            for low in range(0, piece.shape[0], shard):
                row = pl.multiple_of(shard_of(here, blocks[at // shard], planes) * shard, shard)
                mine = refs[N.rows][at:at + shard, :] if at < first else acc[at - first:at - first + shard, :]
                high = mine.astype(BF16)
                whole[0, pl.ds(row, shard), :] = high
                whole[1, pl.ds(row, shard), :] = (mine - high.astype(F32)).astype(BF16)
                whole[2, pl.ds(row, shard), :] = piece[low:low + shard, pl.ds(left, own)]
                at += shard
        half = lax.dot_general(whole[2], whole[0], (((1,), (1,)), ((), ())), preferred_element_type=F32)
        half += lax.dot_general(whole[2], whole[1], (((1,), (1,)), ((), ())), preferred_element_type=F32)
        total[...] = (half + half.T) * scale
        keep, give = cut(total, lax.rem(here, 2), tokens // 2)
        refs[N.mine][...] = keep
        refs[N.other][...] = give

    out = ((tokens // 2, tokens), F32)
    found = call(
        body, place,
        {**dict(enumerate(pieces)), N.rows: rows, N.near: near, **{(N.far, i): e for i, e in enumerate(earlier)}},
        {N.mine: out, N.other: out},
        scratch=[pltpu.VMEM((3, tokens, own), BF16), pltpu.VMEM((tokens, tokens), F32)],
        limit=16 * MIB, far=[(N.far, i) for i in range(len(earlier))],
        flops=2 * tokens * own * tokens, bytes_accessed=2 * own * tokens,
    )
    return found[N.mine], found[N.other]


def fetch(output_factor, place, earlier):
    def body(here, refs, sem):
        copy = pltpu.make_async_copy(refs[N.factor], refs[N.out], sem)
        copy.start()
        copy.wait()

    return call(
        body, place, {N.factor: output_factor, N.earlier: earlier}, {N.out: (output_factor.shape, F32)},
        scratch=[pltpu.SemaphoreType.DMA], limit=MIB, far=(N.factor, N.earlier),
    )[N.out]


def cut(value, which, rows):
    return (
        value[pl.ds(pl.multiple_of(which * rows, rows), rows), :],
        value[pl.ds(pl.multiple_of((1 - which) * rows, rows), rows), :],
    )


def update(pieces, groups, halves, output_factor, place, planes, slab_width):
    rows, columns = output_factor.shape
    blocks = token_blocks(groups)
    tokens = sum(p.shape[0] for p in pieces)
    shard = tokens // len(blocks)
    chunk = min(1024, columns)
    scale = 1.0 / tokens
    half = tokens // 2
    count = len(pieces)

    def body(place_ref, *refs):
        ins = refs[:count]
        mine_ref, other_ref, factor_ref, out_ref, gram, grads, left_abs, left = refs[count:]
        here = place_ref[0]

        @pl.when(pl.program_id(0) == 0)
        def _():
            core = lax.rem(here, 2)
            gram[pl.ds(pl.multiple_of(core * half, half), half), :] = mine_ref[...]
            gram[pl.ds(pl.multiple_of((1 - core) * half, half), half), :] = other_ref[...]
            at = 0
            for piece in ins:
                for low in range(0, piece.shape[0], shard):
                    row = pl.multiple_of(shard_of(here, blocks[at], planes) * shard, shard)
                    grads[pl.ds(row, shard), :] = piece[low:low + shard, slab_width:]
                    at += 1
            left_abs[...] = jnp.dot(gram[...], grads[...], preferred_element_type=F32).astype(BF16)
            order = []
            for block in blocks:
                row = pl.multiple_of(shard_of(here, block, planes) * shard, shard)
                order.append(left_abs[pl.ds(row, shard), :])
            left[...] = jnp.concatenate(order, 0).T

        at = pl.ds(pl.multiple_of(pl.program_id(0) * chunk, chunk), chunk)
        part = jnp.concatenate([p[:, at] for p in ins], 0)
        base = factor_ref[:, at] if FETCH else factor_ref[...]
        out_ref[...] = base + jnp.dot(left[...], part, preferred_element_type=F32) * scale

    vmem = pl.BlockSpec(memory_space=pltpu.VMEM)
    return pl.pallas_call(
        body,
        grid=(columns // chunk,),
        in_specs=[pl.BlockSpec(memory_space=pltpu.SMEM)] + [vmem] * (count + 2)
        + [vmem if FETCH else pl.BlockSpec((rows, chunk), lambda j: (0, j))],
        out_specs=pl.BlockSpec((rows, chunk), lambda j: (0, j)),
        scratch_shapes=[
            pltpu.VMEM((tokens, tokens), BF16), pltpu.VMEM((tokens, rows), BF16), pltpu.VMEM((tokens, rows), BF16),
            pltpu.VMEM((rows, tokens), BF16),
        ],
        out_shape=jax.ShapeDtypeStruct((rows, columns), F32),
        compiler_params=pltpu.CompilerParams(vmem_limit_bytes=UPDATE_VMEM),
        cost_estimate=pl.CostEstimate(
            flops=2 * rows * tokens * (columns + tokens), bytes_accessed=8 * rows * columns, transcendentals=0
        ),
    )(place, *pieces, *halves, output_factor)


def per_device(inputs, input_factor, out_grads, output_factor):
    n = lax.axis_size("row")
    planes = n // 4
    half = planes // 2
    place = lax.axis_index("row").reshape(1)
    near = sorted((k for k in range(1, planes) if k != half), key=lambda k: min(k, planes - k))
    early, late = near[: len(near) // 2], near[len(near) // 2:]
    rows, features = inputs.shape
    width, used = features // planes, half + 1
    x_width = half * width + width // 2
    slab_width = output_factor.shape[1]
    own_width = out_grads.shape[1] // n
    cross_width = slab_width + 2 * own_width
    pair_width = slab_width + own_width
    x_shape = ((rows, x_width), BF16)

    def across(value):
        return permute(value, y_perm(n))

    def other_core(value):
        return permute(value, core_perm(n))

    def ahead(value, k):
        return permute(value, plane_perm(n, k))

    def y_of(here):
        return lax.rem(here // 2, 2)

    def columns(ref, first, count, size):
        return ref[:, pl.ds(pl.multiple_of(first * size, size), count * size)]

    def take(out, row, ref, here, other):
        size = width // 2
        out[row:row + rows, : half * width] = ref[:, : half * width]
        left = pl.multiple_of(half * width + half_block(here, planes, other) * size, size)
        out[row:row + rows, half * width:] = ref[:, pl.ds(left, size)]

    def grads_ahead(grads, here, k):
        return columns(grads, lax.rem(here // 4 + k, planes), 1, 4 * own_width)

    def for_neighbour(ref, here):
        return columns(ref, 1 - y_of(here), 1, 2 * own_width)

    def pair(own, give, row, slab, grads, here):
        core = lax.rem(here, 2)
        for out, c in ((own, core), (give, 1 - core)):
            out[row:row + rows, :slab_width] = slab
            out[row:row + rows, slab_width:] = grads(c)

    def pairs(own, give, here, slabs, slabs_crossed, grads, grads_crossed):
        y = y_of(here)
        for i, ref in enumerate(slabs):
            pair(own, give, i * rows, ref[...], lambda c, i=i: columns(grads[i], y * 2 + c, 1, own_width), here)
        for i in range(len(slabs)):
            at = slice(i * rows, (i + 1) * rows)
            mine = lambda c, at=at: grads_crossed[at, pl.ds(pl.multiple_of(c * own_width, own_width), own_width)]
            pair(own, give, (len(slabs) + i) * rows, slabs_crossed[at, :], mine, here)

    def pair_shapes(count):
        return {k: ((2 * count * rows, pair_width), BF16) for k in (N.own, N.give)}

    slab_shape, grads_shape = ((rows, slab_width), BF16), ((rows, 4 * own_width), BF16)

    blocks = {k: used + (k == half - 1) for k in near}

    def first(here, r):
        plane = here // 4
        for k in near:
            for j in range(blocks[k]):
                r[k][:, j * width:(j + 1) * width] = columns(r[N.x], lax.rem(plane + k + j, planes), 1, width)
        for name, other in ((N.own, False), (N.cross, True)):
            for j in range(half):
                r[name][:, j * width:(j + 1) * width] = columns(r[N.x], lax.rem(plane + j, planes), 1, width)
            at = lax.rem(plane + half, planes) * 2 + half_block(here, planes, other)
            r[name][:, half * width:] = columns(r[N.x], at, 1, width // 2)

    def first_grads(here, r):
        plane = here // 4
        r[N.cross][:, :slab_width] = r[N.grads][:, :slab_width]
        r[N.cross][:, slab_width:] = columns(r[N.grads], plane * 2 + 1 - y_of(here), 1, 2 * own_width)
        r[N.slab][...] = r[N.grads][:, :slab_width]
        r[N.chip][...] = columns(r[N.grads], plane * 2 + y_of(here), 1, 2 * own_width)
        for k in range(1, planes):
            r[k][...] = grads_ahead(r[N.grads], here, k)

    out = call(
        first, place, {N.x: inputs},
        {**{k: ((rows, blocks[k] * width), BF16) for k in near}, N.own: x_shape, N.cross: x_shape},
    )
    own = out[N.own]
    got = {k: ahead(out[k], k) for k in near}
    crossed_0 = across(out[N.cross])
    sent = call(
        first_grads, place, {N.grads: out_grads},
        {
            N.cross: ((rows, cross_width), BF16), N.slab: slab_shape, N.chip: ((rows, 2 * own_width), BF16),
            **{k: grads_shape for k in range(1, planes)},
        },
    )
    grads_crossed_0 = across(sent[N.cross])

    def second(here, r):
        r[N.far][...] = r[half - 1][:, width:]
        for i, k in enumerate(near):
            take(r[N.near], i * rows, r[k], here, True)
        stack(r[N.pair], [r[N.own], r[N.crossed]])
        r[N.slab][...] = r[N.sent][...]

    out = call(
        second, place,
        {
            **{k: got[k] for k in near}, N.own: own, N.crossed: crossed_0, N.sent: sent[N.slab],
            N.grads_crossed: grads_crossed_0,
        },
        {
            N.far: ((rows, used * width), BF16), N.near: ((len(near) * rows, x_width), BF16),
            N.pair: ((2 * rows, x_width), BF16), N.slab: slab_shape,
        },
        far=(N.grads_crossed,),
    )
    pair_0 = out[N.pair]
    far = ahead(out[N.far], 1)
    crossed_near = across(out[N.near])
    pair_0_other = other_core(pair_0)
    slab_got = {k: ahead(out[N.slab], k) for k in early}

    def third(here, r):
        take(r[N.cross], 0, r[N.far], here, True)
        for i, k in enumerate(near):
            take(r[N.pair], i * rows, r[k], here, False)
        r[N.pair][len(near) * rows:, :] = r[N.crossed][...]
        stack(r[N.slab_cross], [r[N.slab, k] for k in early])
        r[N.slab][...] = r[N.sent][...]
        for k in near:
            r[N.send, k][...] = r[N.sent, k][...]

    out = call(
        third, place,
        {
            **{k: got[k] for k in near}, N.far: far, N.crossed: crossed_near, N.other: pair_0_other,
            N.sent: sent[N.slab], **{(N.sent, k): sent[k] for k in near}, **{(N.slab, k): slab_got[k] for k in early},
        },
        {
            N.cross: x_shape, N.pair: ((2 * len(near) * rows, x_width), BF16),
            N.slab_cross: ((len(early) * rows, slab_width), BF16), N.slab: slab_shape,
            **{(N.send, k): grads_shape for k in near},
        },
    )
    pair_near = out[N.pair]
    crossed_far = across(out[N.cross])
    pair_near_other = other_core(pair_near)
    grads_got = {k: ahead(out[N.send, k], k) for k in near}
    slab_got.update({k: ahead(out[N.slab], k) for k in late})
    slab_early_crossed = across(out[N.slab_cross])
    before = [pair_0, pair_0_other, pair_near, pair_near_other]
    products, blocks_here = gram_rows(before, input_factor, place, planes)

    def fourth(here, r):
        take(r[N.pair], 0, r[N.far], here, False)
        r[N.pair][rows:, :] = r[N.crossed][...]
        r[N.slab][...] = r[N.between][...]
        r[N.send][...] = r[N.sent][...]

    out = call(
        fourth, place,
        {
            N.far: far, N.crossed: crossed_far, N.other: pair_near_other, N.between: slab_got[half - 1],
            N.sent: sent[half], N.products: products, **{(N.grads, k): grads_got[k] for k in near},
            **{(N.late, k): slab_got[k] for k in late},
        },
        {N.pair: ((2 * rows, x_width), BF16), N.slab: slab_shape, N.send: grads_shape},
        far=(N.products, *[(N.grads, k) for k in near], *[(N.late, k) for k in late]),
    )
    after = [out[N.pair], other_core(out[N.pair])]
    far_slab = ahead(out[N.slab], 1)
    far_grads = ahead(out[N.send], half)

    def own_pair(here, r):
        mine = lambda c: columns(r[N.chip], c, 1, own_width)
        pair(r[N.own], r[N.give], 0, r[N.slab][...], mine, here)
        mine = lambda c: r[N.crossed][:, pl.ds(pl.multiple_of(slab_width + c * own_width, 128), own_width)]
        pair(r[N.own], r[N.give], rows, r[N.crossed][:, :slab_width], mine, here)

    out = call(
        own_pair, place, {N.slab: sent[N.slab], N.chip: sent[N.chip], N.crossed: grads_crossed_0}, pair_shapes(1)
    )
    final = [out[N.own], other_core(out[N.give])]
    mine, other = gram_part(products, blocks_here, before, after, [[0], near, [half]], place, planes, features, [])
    tokens = mine.shape[1]
    other = other_core(other)

    quarter = tokens // 4

    def fifth(here, r, total):
        total[...] = r[N.mine][...] + r[N.other][...]
        keep, give = cut(total, y_of(here), quarter)
        r[N.keep][...] = keep
        r[N.low][...] = give.astype(BF16)

    out = call(
        fifth, place, {N.mine: mine, N.other: other},
        {N.keep: ((quarter, tokens), F32), N.low: ((quarter, tokens), BF16)},
        scratch=[pltpu.VMEM((2 * quarter, tokens), F32)],
    )
    total, low = out[N.keep], across(out[N.low])

    def add(here, r):
        total = r[N.mine][...] + r[N.other][...].astype(F32)
        r[N.sum][...] = total
        r[N.low][...] = total.astype(BF16)

    def add_near(here, r):
        add(here, r)
        stack(r[N.slab_cross], [r[N.slab, k] for k in late])
        for i, k in enumerate(near):
            r[N.grads_cross][i * rows:(i + 1) * rows, :] = for_neighbour(r[N.grads, k], here)

    shapes = {N.sum: (total.shape, F32), N.low: (total.shape, BF16)}
    out = call(
        add_near, place,
        {
            N.mine: total, N.other: low, **{(N.slab, k): slab_got[k] for k in late},
            **{(N.grads, k): grads_got[k] for k in near},
        },
        {
            **shapes, N.slab_cross: ((len(late) * rows, slab_width), BF16),
            N.grads_cross: ((len(near) * rows, 2 * own_width), BF16),
        },
    )
    slab_late_crossed, grads_crossed = across(out[N.slab_cross]), across(out[N.grads_cross])
    factor = fetch(output_factor, place, out[N.sum])

    def far_slab_across(here, r):
        r[N.cross][...] = r[N.slab][...]

    def far_grads_across(here, r):
        r[N.cross][...] = for_neighbour(r[N.grads], here)

    step = 4
    while step < n:
        low = permute(out[N.low], [(i, i ^ step) for i in range(n)])
        ins = {N.mine: out[N.sum], N.other: low}
        if step == 4:
            out = call(
                add, place, {**ins, N.factor: factor, N.late: slab_late_crossed, N.near: grads_crossed, N.far_slab: far_slab}, shapes,
                far=(N.factor, N.late, N.near, N.far_slab),
            )
            far_sent = call(
                far_slab_across, place, {N.slab: far_slab, N.earlier: out[N.sum]}, {N.cross: slab_shape}, far=(N.earlier,)
            )
        else:
            out = call(add, place, ins, shapes)
        step *= 2
    far_slab_crossed = across(far_sent[N.cross])
    summed = out[N.sum]
    far_sent = call(
        far_grads_across, place, {N.grads: far_grads, N.earlier: summed},
        {N.cross: ((rows, 2 * own_width), BF16)}, far=(N.earlier,),
    )
    far_grads_crossed = across(far_sent[N.cross])

    def near_pairs(here, r):
        groups = ((early, r[N.early], 0), (late, r[N.late], len(early)))
        for i, (some, crossed, at) in enumerate(groups):
            pairs(
                r[N.own, i], r[N.give, i], here, [r[N.slab, k] for k in some], crossed, [r[N.grads, k] for k in some],
                r[N.grads_crossed].at[at * rows:(at + len(some)) * rows, :],
            )

    pair_out = call(
        near_pairs, place,
        {
            N.early: slab_early_crossed, N.late: slab_late_crossed, N.grads_crossed: grads_crossed,
            **{(N.slab, k): slab_got[k] for k in near}, **{(N.grads, k): grads_got[k] for k in near}, N.earlier: summed,
        },
        {(k, i): shape for i, some in enumerate((early, late)) for k, shape in pair_shapes(len(some)).items()},
        far=(N.earlier,),
    )
    for i in range(2):
        final += [pair_out[N.own, i], other_core(pair_out[N.give, i])]

    low = out[N.low]

    def join(here, r):
        y = y_of(here)
        r[N.gram][pl.ds(pl.multiple_of(y * quarter, quarter), quarter), :] = r[N.mine][...]
        r[N.gram][pl.ds(pl.multiple_of((1 - y) * quarter, quarter), quarter), :] = r[N.other][...]

    out = call(join, place, {N.mine: low, N.other: across(low)}, {N.gram: ((2 * quarter, tokens), BF16)})
    halves = [out[N.gram], other_core(out[N.gram])]

    def last(here, r):
        pairs(r[N.own], r[N.give], here, [r[N.slab]], r[N.slabs], [r[N.grads]], r[N.crossed])

    out = call(
        last, place,
        {
            N.slab: far_slab, N.slabs: far_slab_crossed, N.grads: far_grads, N.crossed: far_grads_crossed,
            N.earlier: out[N.gram],
        },
        pair_shapes(1), far=(N.earlier,),
    )
    final += [out[N.own], other_core(out[N.give])]
    return update(final, [[0], early, late, [half]], halves, factor, place, planes, slab_width)


def solution(mesh):
    spec = P(("groups", "row"), None)
    return jax.shard_map(per_device, mesh=mesh, in_specs=(spec,) * 4, out_specs=spec, check_vma=False)
```

```python
import enum

import jax
import jax.numpy as jnp
from jax import lax
from jax.experimental import pallas as pl
from jax.experimental.pallas import tpu as pltpu
from jax.sharding import PartitionSpec as P

BF16 = jnp.bfloat16
F32 = jnp.float32
MIB = 1024 * 1024
GRAM_ROWS_VMEM = 44 * MIB
UPDATE_VMEM = 22 * MIB
FETCH = True


class N(enum.Enum):
    near = enum.auto()
    rows = enum.auto()
    factor = enum.auto()
    mine = enum.auto()
    other = enum.auto()
    low = enum.auto()
    far = enum.auto()
    out = enum.auto()
    earlier = enum.auto()
    own = enum.auto()
    give = enum.auto()
    x = enum.auto()
    cross = enum.auto()
    grads = enum.auto()
    slab = enum.auto()
    chip = enum.auto()
    pair = enum.auto()
    crossed = enum.auto()
    sent = enum.auto()
    grads_crossed = enum.auto()
    slab_cross = enum.auto()
    send = enum.auto()
    products = enum.auto()
    rest = enum.auto()
    keep = enum.auto()
    sum = enum.auto()
    gram = enum.auto()
    slabs = enum.auto()


def permute(value, perm):
    return lax.ppermute(value, "row", perm)


def core_perm(n):
    return [(i, i ^ 1) for i in range(n)]


def y_perm(n):
    return [(i, i ^ 2) for i in range(n)]


def plane_perm(n, step):
    return [(i, (i + 4 * step) % n) for i in range(n)]


def call(body, place, inputs, outputs, scratch=(), limit=4 * MIB, flops=0, bytes_accessed=0, far=()):
    vmem = pl.BlockSpec(memory_space=pltpu.VMEM)
    anywhere = pl.BlockSpec(memory_space=pltpu.HBM)
    names = [*inputs, *outputs]

    def kernel(place_ref, *refs):
        body(place_ref[0], dict(zip(names, refs)), *refs[len(names):])

    results = pl.pallas_call(
        kernel,
        in_specs=[pl.BlockSpec(memory_space=pltpu.SMEM)] + [anywhere if k in far else vmem for k in inputs],
        out_specs=[vmem] * len(outputs),
        out_shape=[jax.ShapeDtypeStruct(shape, dtype) for shape, dtype in outputs.values()],
        scratch_shapes=list(scratch),
        compiler_params=pltpu.CompilerParams(vmem_limit_bytes=limit),
        cost_estimate=pl.CostEstimate(flops=flops, bytes_accessed=bytes_accessed, transcendentals=0),
    )(place, *inputs.values())
    return dict(zip(outputs, results))


def stack(out, refs):
    row = 0
    for ref in refs:
        out[row:row + ref.shape[0], :] = ref[...]
        row += ref.shape[0]


def token_blocks(groups):
    return [(k, y, core) for group in groups for core in (0, 1) for y in (0, 1) for k in group]


def shard_of(place, block, planes):
    back, other_y, other_core = block
    plane = lax.rem(place // 4 + planes - back, planes)
    y, core = lax.rem(place // 2, 2), lax.rem(place, 2)
    return plane * 4 + (1 - y if other_y else y) * 2 + (1 - core if other_core else core)


def half_block(place, planes, other):
    y = lax.rem(place // 2, 2)
    y = 1 - y if other else y
    return jnp.where(place // 4 < planes // 2, y, 1 - y)


def gram_rows(pieces, input_factor, place, planes):
    own, features = input_factor.shape
    width = features // planes
    half = planes // 2
    columns = pieces[0].shape[1]
    tokens = sum(p.shape[0] for p in pieces)
    count = len(pieces)

    def body(here, refs, sems):
        near, acc = refs[N.near], refs[N.rows]
        copies = []
        for j in range(half + 1):
            left = lax.rem(here // 4 + j, planes) * width
            size = width
            if j == half:
                size = width // 2
                left = left + half_block(here, planes, False) * size
            copies.append(
                pltpu.make_async_copy(
                    refs[N.factor].at[:, pl.ds(pl.multiple_of(left, size), size)],
                    near.at[:, j * width:j * width + size], sems.at[j],
                )
            )
            copies[-1].start()
        for j, copy in enumerate(copies):
            copy.wait()
            at = slice(j * width, min((j + 1) * width, columns))
            rows = jnp.concatenate([refs[i][:, at] for i in range(count)], 0)
            part = lax.dot_general(rows, near[:, at], (((1,), (1,)), ((), ())), preferred_element_type=F32)
            acc[...] = part * 0.5 if j == 0 else acc[...] + part

    out = call(
        body, place, {**dict(enumerate(pieces)), N.factor: input_factor},
        {N.rows: ((tokens, own), F32), N.near: ((own, columns), input_factor.dtype)},
        scratch=[pltpu.SemaphoreType.DMA((half + 1,))], limit=GRAM_ROWS_VMEM, far=(N.factor,),
        flops=2 * tokens * own * columns, bytes_accessed=2 * own * columns,
    )
    return out[N.rows], out[N.near]


def gram_part(rows, near, before, after, groups, place, planes, features, earlier):
    own, columns = near.shape
    width = features // planes
    blocks = token_blocks(groups)
    pieces = [*before, *after]
    tokens = sum(p.shape[0] for p in pieces)
    shard = tokens // len(blocks)
    count = len(pieces)
    scale = float(features) ** -0.5

    def body(here, refs, whole, total):
        ins = [refs[i] for i in range(count)]
        last = jnp.concatenate([refs[i][...] for i in range(len(before), count)], 0)
        near = refs[N.near]
        acc = 0.5 * lax.dot_general(
            last[:, :width], near[:, :width], (((1,), (1,)), ((), ())), preferred_element_type=F32
        )
        acc += lax.dot_general(last[:, width:], near[:, width:], (((1,), (1,)), ((), ())), preferred_element_type=F32)
        left = pl.multiple_of(lax.rem(here, 4) * own, own)
        at, first = 0, refs[N.rows].shape[0]
        for piece in ins:
            for low in range(0, piece.shape[0], shard):
                row = pl.multiple_of(shard_of(here, blocks[at // shard], planes) * shard, shard)
                mine = refs[N.rows][at:at + shard, :] if at < first else acc[at - first:at - first + shard, :]
                high = mine.astype(BF16)
                whole[0, pl.ds(row, shard), :] = high
                whole[1, pl.ds(row, shard), :] = (mine - high.astype(F32)).astype(BF16)
                whole[2, pl.ds(row, shard), :] = piece[low:low + shard, pl.ds(left, own)]
                at += shard
        half = lax.dot_general(whole[2], whole[0], (((1,), (1,)), ((), ())), preferred_element_type=F32)
        half += lax.dot_general(whole[2], whole[1], (((1,), (1,)), ((), ())), preferred_element_type=F32)
        total[...] = (half + half.T) * scale
        keep, give = cut(total, lax.rem(here, 2), tokens // 2)
        refs[N.mine][...] = keep
        high = give.astype(BF16)
        refs[N.other][...] = high
        refs[N.low][...] = (give - high.astype(F32)).astype(BF16)

    out = (tokens // 2, tokens)
    found = call(
        body, place,
        {**dict(enumerate(pieces)), N.rows: rows, N.near: near, **{(N.far, i): e for i, e in enumerate(earlier)}},
        {N.mine: (out, F32), N.other: (out, BF16), N.low: (out, BF16)},
        scratch=[pltpu.VMEM((3, tokens, own), BF16), pltpu.VMEM((tokens, tokens), F32)],
        limit=16 * MIB, far=[(N.far, i) for i in range(len(earlier))],
        flops=2 * tokens * own * tokens, bytes_accessed=2 * own * tokens,
    )
    return found[N.mine], found[N.other], found[N.low]


def fetch(output_factor, place, earlier):
    def body(here, refs, sem):
        copy = pltpu.make_async_copy(refs[N.factor], refs[N.out], sem)
        copy.start()
        copy.wait()

    return call(
        body, place, {N.factor: output_factor, N.earlier: earlier}, {N.out: (output_factor.shape, F32)},
        scratch=[pltpu.SemaphoreType.DMA], limit=MIB, far=(N.factor, N.earlier),
    )[N.out]


def cut(value, which, rows):
    return (
        value[pl.ds(pl.multiple_of(which * rows, rows), rows), :],
        value[pl.ds(pl.multiple_of((1 - which) * rows, rows), rows), :],
    )


def update(pieces, groups, halves, output_factor, place, planes, slab_width):
    rows, columns = output_factor.shape
    blocks = token_blocks(groups)
    tokens = sum(p.shape[0] for p in pieces)
    shard = tokens // len(blocks)
    chunk = min(1024, columns)
    scale = 1.0 / tokens
    half = tokens // 2
    count = len(pieces)

    def body(place_ref, *refs):
        ins = refs[:count]
        mine_ref, other_ref, factor_ref, out_ref, gram, grads, left_abs, left = refs[count:]
        here = place_ref[0]

        @pl.when(pl.program_id(0) == 0)
        def _():
            core = lax.rem(here, 2)
            gram[pl.ds(pl.multiple_of(core * half, half), half), :] = mine_ref[...]
            gram[pl.ds(pl.multiple_of((1 - core) * half, half), half), :] = other_ref[...]
            at = 0
            for piece in ins:
                for low in range(0, piece.shape[0], shard):
                    row = pl.multiple_of(shard_of(here, blocks[at], planes) * shard, shard)
                    grads[pl.ds(row, shard), :] = piece[low:low + shard, slab_width:]
                    at += 1
            left_abs[...] = jnp.dot(gram[...], grads[...], preferred_element_type=F32).astype(BF16)
            order = []
            for block in blocks:
                row = pl.multiple_of(shard_of(here, block, planes) * shard, shard)
                order.append(left_abs[pl.ds(row, shard), :])
            left[...] = jnp.concatenate(order, 0).T

        at = pl.ds(pl.multiple_of(pl.program_id(0) * chunk, chunk), chunk)
        part = jnp.concatenate([p[:, at] for p in ins], 0)
        base = factor_ref[:, at] if FETCH else factor_ref[...]
        out_ref[...] = base + jnp.dot(left[...], part, preferred_element_type=F32) * scale

    vmem = pl.BlockSpec(memory_space=pltpu.VMEM)
    return pl.pallas_call(
        body,
        grid=(columns // chunk,),
        in_specs=[pl.BlockSpec(memory_space=pltpu.SMEM)] + [vmem] * (count + 2)
        + [vmem if FETCH else pl.BlockSpec((rows, chunk), lambda j: (0, j))],
        out_specs=pl.BlockSpec((rows, chunk), lambda j: (0, j)),
        scratch_shapes=[
            pltpu.VMEM((tokens, tokens), BF16), pltpu.VMEM((tokens, rows), BF16), pltpu.VMEM((tokens, rows), BF16),
            pltpu.VMEM((rows, tokens), BF16),
        ],
        out_shape=jax.ShapeDtypeStruct((rows, columns), F32),
        compiler_params=pltpu.CompilerParams(vmem_limit_bytes=UPDATE_VMEM),
        cost_estimate=pl.CostEstimate(
            flops=2 * rows * tokens * (columns + tokens), bytes_accessed=8 * rows * columns, transcendentals=0
        ),
    )(place, *pieces, *halves, output_factor)


def per_device(inputs, input_factor, out_grads, output_factor):
    n = lax.axis_size("row")
    planes = n // 4
    half = planes // 2
    place = lax.axis_index("row").reshape(1)
    near = sorted((k for k in range(1, planes) if k != half), key=lambda k: (k != half - 1, min(k, planes - k)))
    early, late = near[: len(near) // 2], near[len(near) // 2:]
    rows, features = inputs.shape
    width, used = features // planes, half + 1
    x_width = half * width + width // 2
    slab_width = output_factor.shape[1]
    own_width = out_grads.shape[1] // n
    cross_width = slab_width + 2 * own_width
    pair_width = slab_width + own_width
    x_shape = ((rows, x_width), BF16)

    def across(value):
        return permute(value, y_perm(n))

    def other_core(value):
        return permute(value, core_perm(n))

    def ahead(value, k):
        return permute(value, plane_perm(n, k))

    def y_of(here):
        return lax.rem(here // 2, 2)

    def columns(ref, first, count, size):
        return ref[:, pl.ds(pl.multiple_of(first * size, size), count * size)]

    def take(out, row, ref, here, other):
        size = width // 2
        out[row:row + rows, : half * width] = ref[:, : half * width]
        left = pl.multiple_of(half * width + half_block(here, planes, other) * size, size)
        out[row:row + rows, half * width:] = ref[:, pl.ds(left, size)]

    def grads_ahead(grads, here, k):
        return columns(grads, lax.rem(here // 4 + k, planes), 1, 4 * own_width)

    def for_neighbour(ref, here, low=0):
        return ref[:, pl.ds(pl.multiple_of(low + (1 - y_of(here)) * 2 * own_width, own_width), 2 * own_width)]

    def pair(own, give, row, slab, grads, here):
        core = lax.rem(here, 2)
        for out, c in ((own, core), (give, 1 - core)):
            out[row:row + rows, :slab_width] = slab
            out[row:row + rows, slab_width:] = grads(c)

    def pairs(own, give, here, slabs, slabs_crossed, grads, lows, grads_crossed):
        y = y_of(here)
        for i, ref in enumerate(slabs):
            mine = lambda c, i=i: grads[i][
                :, pl.ds(pl.multiple_of(lows[i] + (y * 2 + c) * own_width, own_width), own_width)
            ]
            pair(own, give, i * rows, ref[:, :slab_width], mine, here)
        for i in range(len(slabs)):
            at = slice(i * rows, (i + 1) * rows)
            mine = lambda c, at=at: grads_crossed[at, pl.ds(pl.multiple_of(c * own_width, own_width), own_width)]
            pair(own, give, (len(slabs) + i) * rows, slabs_crossed[at, :], mine, here)

    def pair_shapes(count):
        return {k: ((2 * count * rows, pair_width), BF16) for k in (N.own, N.give)}

    slab_shape, grads_shape = ((rows, slab_width), BF16), ((rows, 4 * own_width), BF16)
    wide_shape = ((rows, slab_width + 4 * own_width), BF16)
    together = half - 1 == 1

    blocks = {k: used + (k == half - 1) for k in near}

    def first(here, r):
        plane = here // 4
        for k in near:
            for j in range(blocks[k]):
                r[k][:, j * width:(j + 1) * width] = columns(r[N.x], lax.rem(plane + k + j, planes), 1, width)
        for name, other in ((N.own, False), (N.cross, True)):
            for j in range(half):
                r[name][:, j * width:(j + 1) * width] = columns(r[N.x], lax.rem(plane + j, planes), 1, width)
            at = lax.rem(plane + half, planes) * 2 + half_block(here, planes, other)
            r[name][:, half * width:] = columns(r[N.x], at, 1, width // 2)

    def first_grads(here, r):
        plane = here // 4
        r[N.cross][:, :slab_width] = r[N.grads][:, :slab_width]
        r[N.cross][:, slab_width:] = columns(r[N.grads], plane * 2 + 1 - y_of(here), 1, 2 * own_width)
        r[N.slab][...] = r[N.grads][:, :slab_width]
        r[N.chip][...] = columns(r[N.grads], plane * 2 + y_of(here), 1, 2 * own_width)
        for k in range(1, planes):
            r[k][...] = grads_ahead(r[N.grads], here, k)

    out = call(
        first, place, {N.x: inputs},
        {**{k: ((rows, blocks[k] * width), BF16) for k in near}, N.own: x_shape, N.cross: x_shape},
    )
    own = out[N.own]
    got = {k: ahead(out[k], k) for k in near}
    crossed_0 = across(out[N.cross])
    sent = call(
        first_grads, place, {N.grads: out_grads},
        {
            N.cross: ((rows, cross_width), BF16), N.slab: slab_shape, N.chip: ((rows, 2 * own_width), BF16),
            **{k: grads_shape for k in range(1, planes)},
        },
    )
    grads_crossed_0 = across(sent[N.cross])

    def second(here, r):
        r[N.far][...] = r[half - 1][:, width:]
        for i, k in enumerate(near):
            take(r[N.near], i * rows, r[k], here, True)
        stack(r[N.pair], [r[N.own], r[N.crossed]])
        r[N.slab][...] = r[N.sent][...]

    out = call(
        second, place,
        {
            **{k: got[k] for k in near}, N.own: own, N.crossed: crossed_0, N.sent: sent[N.slab],
            N.grads_crossed: grads_crossed_0,
        },
        {
            N.far: ((rows, used * width), BF16), N.near: ((len(near) * rows, x_width), BF16),
            N.pair: ((2 * rows, x_width), BF16), N.slab: slab_shape,
        },
        far=(N.grads_crossed,),
    )
    pair_0 = out[N.pair]
    far = ahead(out[N.far], 1)
    crossed_near = across(out[N.near])
    pair_0_other = other_core(pair_0)
    slab_got = {k: ahead(out[N.slab], k) for k in early}

    def third(here, r):
        take(r[N.cross], 0, r[N.far], here, True)
        for i, k in enumerate(near):
            take(r[N.pair], i * rows, r[k], here, False)
        r[N.pair][len(near) * rows:, :] = r[N.crossed][...]
        stack(r[N.slab_cross], [r[N.slab, k] for k in early])
        for k in early:
            if together and k == half - 1:
                r[N.send, k][:, :slab_width] = r[N.slab, k][...]
                r[N.send, k][:, slab_width:] = r[N.sent, k][...]
            else:
                r[N.send, k][...] = r[N.sent, k][...]
        if not together:
            r[N.slab][...] = r[N.slab, half - 1][...]

    out = call(
        third, place,
        {
            **{k: got[k] for k in near}, N.far: far, N.crossed: crossed_near, N.other: pair_0_other,
            **{(N.sent, k): sent[k] for k in early}, **{(N.slab, k): slab_got[k] for k in early},
        },
        {
            N.cross: x_shape, N.pair: ((2 * len(near) * rows, x_width), BF16),
            N.slab_cross: ((len(early) * rows, slab_width), BF16), **({} if together else {N.slab: slab_shape}),
            **{(N.send, k): wide_shape if together and k == half - 1 else grads_shape for k in early},
        },
    )
    pair_near = out[N.pair]
    crossed_far = across(out[N.cross])
    pair_near_other = other_core(pair_near)
    grads_got = {k: (ahead(out[N.send, k], k), slab_width if together and k == half - 1 else 0) for k in early}
    far_slab = grads_got[half - 1][0] if together else ahead(out[N.slab], 1)
    slab_early_crossed = across(out[N.slab_cross])
    before = [pair_0, pair_0_other, pair_near, pair_near_other]
    products, blocks_here = gram_rows(before, input_factor, place, planes)

    def fourth(here, r):
        take(r[N.pair], 0, r[N.far], here, False)
        r[N.pair][rows:, :] = r[N.crossed][...]
        r[N.send][...] = r[N.sent, half][...]
        for k in late:
            r[N.send, k][:, :slab_width] = r[N.sent][...]
            r[N.send, k][:, slab_width:] = r[N.sent, k][...]

    out = call(
        fourth, place,
        {
            N.far: far, N.crossed: crossed_far, N.other: pair_near_other, N.products: products,
            N.sent: sent[N.slab], **{(N.sent, k): sent[k] for k in [*late, half]},
            **{(N.grads, k): grads_got[k][0] for k in early}, N.slab_cross: slab_early_crossed,
        },
        {N.pair: ((2 * rows, x_width), BF16), N.send: grads_shape, **{(N.send, k): wide_shape for k in late}},
        far=(N.products, N.slab_cross, *[(N.grads, k) for k in early]),
    )
    after = [out[N.pair], other_core(out[N.pair])]
    for k in late:
        slab_got[k] = ahead(out[N.send, k], k)
        grads_got[k] = (slab_got[k], slab_width)
    far_grads = ahead(out[N.send], half)

    def own_pair(here, r):
        mine = lambda c: columns(r[N.chip], c, 1, own_width)
        pair(r[N.own], r[N.give], 0, r[N.slab][...], mine, here)
        mine = lambda c: r[N.crossed][:, pl.ds(pl.multiple_of(slab_width + c * own_width, 128), own_width)]
        pair(r[N.own], r[N.give], rows, r[N.crossed][:, :slab_width], mine, here)

    out = call(
        own_pair, place, {N.slab: sent[N.slab], N.chip: sent[N.chip], N.crossed: grads_crossed_0}, pair_shapes(1)
    )
    final = [out[N.own], other_core(out[N.give])]
    mine, other, rest = gram_part(products, blocks_here, before, after, [[0], near, [half]], place, planes, features, [])
    tokens = mine.shape[1]
    other, rest = other_core(other), other_core(rest)

    quarter = tokens // 4

    def fifth(here, r, total):
        total[...] = r[N.mine][...] + (r[N.other][...].astype(F32) + r[N.rest][...].astype(F32))
        keep, give = cut(total, y_of(here), quarter)
        r[N.keep][...] = keep
        r[N.low][...] = give.astype(BF16)

    out = call(
        fifth, place, {N.mine: mine, N.other: other, N.rest: rest},
        {N.keep: ((quarter, tokens), F32), N.low: ((quarter, tokens), BF16)},
        scratch=[pltpu.VMEM((2 * quarter, tokens), F32)],
    )
    total, low = out[N.keep], across(out[N.low])

    def late_across(here, r):
        for i, k in enumerate(late):
            at = slice(i * rows, (i + 1) * rows)
            r[N.cross][at, :slab_width] = r[N.grads, k][:, :slab_width]
            r[N.cross][at, slab_width:] = for_neighbour(r[N.grads, k], here, grads_got[k][1])

    mixed_shape = ((len(late) * rows, cross_width), BF16)
    late_out = call(
        late_across, place,
        {N.earlier: out[N.low], **{(N.grads, k): grads_got[k][0] for k in late}},
        {N.cross: mixed_shape}, far=(N.earlier,),
    )
    mixed_crossed = across(late_out[N.cross])

    def add(here, r):
        total = r[N.mine][...] + r[N.other][...].astype(F32)
        r[N.sum][...] = total
        r[N.low][...] = total.astype(BF16)

    def add_near(here, r):
        add(here, r)
        for i, k in enumerate(early):
            at = slice(i * rows, (i + 1) * rows)
            r[N.cross][at, slab_width:] = for_neighbour(r[N.grads, k], here, grads_got[k][1])
        r[N.cross][:rows, :slab_width] = r[N.slab][:, :slab_width]

    shapes = {N.sum: (total.shape, F32), N.low: (total.shape, BF16)}
    out = call(
        add_near, place,
        {
            N.mine: total, N.other: low, N.slab: far_slab, N.earlier: late_out[N.cross],
            **{(N.grads, k): grads_got[k][0] for k in early},
        },
        {**shapes, N.cross: mixed_shape}, far=(N.earlier,),
    )
    far_mixed_crossed = across(out[N.cross])
    factor = fetch(output_factor, place, out[N.sum])
    def far_grads_across(here, r):
        r[N.cross][...] = for_neighbour(r[N.grads], here)

    step = 4
    while step < n:
        low = permute(out[N.low], [(i, i ^ step) for i in range(n)])
        ins = {N.mine: out[N.sum], N.other: low}
        if step == 4:
            ins.update({N.factor: factor, N.crossed: far_mixed_crossed, N.grads: far_grads})
            out = call(add, place, ins, shapes, far=(N.factor, N.crossed, N.grads))
        else:
            out = call(add, place, {**ins, N.crossed: mixed_crossed}, shapes, far=(N.crossed,))
        step *= 2
    summed = out[N.sum]
    far_sent = call(
        far_grads_across, place, {N.grads: far_grads, N.earlier: summed},
        {N.cross: ((rows, 2 * own_width), BF16)}, far=(N.earlier,),
    )
    far_grads_crossed = across(far_sent[N.cross])

    def near_pairs(here, r):
        mixed, far_mixed = r[N.crossed], r[N.far]
        sources = (
            (early, r[N.slab], far_mixed.at[:, slab_width:]),
            (late, mixed.at[:, :slab_width], mixed.at[:, slab_width:]),
        )
        for i, (some, slabs, crossed) in enumerate(sources):
            own_slabs = [r[N.slab, k] if k in early else r[N.grads, k] for k in some]
            grads = [r[N.grads, k] for k in some]
            pairs(r[N.own, i], r[N.give, i], here, own_slabs, slabs, grads, [grads_got[k][1] for k in some], crossed)

    pair_out = call(
        near_pairs, place,
        {
            N.slab: slab_early_crossed, N.crossed: mixed_crossed, N.far: far_mixed_crossed, N.earlier: summed,
            **{(N.slab, k): slab_got[k] for k in early}, **{(N.grads, k): grads_got[k][0] for k in near},
        },
        {(k, i): shape for i, some in enumerate((early, late)) for k, shape in pair_shapes(len(some)).items()},
        far=(N.earlier,),
    )
    for i in range(2):
        final += [pair_out[N.own, i], other_core(pair_out[N.give, i])]

    low = out[N.low]

    def join(here, r):
        y = y_of(here)
        r[N.gram][pl.ds(pl.multiple_of(y * quarter, quarter), quarter), :] = r[N.mine][...]
        r[N.gram][pl.ds(pl.multiple_of((1 - y) * quarter, quarter), quarter), :] = r[N.other][...]

    out = call(join, place, {N.mine: low, N.other: across(low)}, {N.gram: ((2 * quarter, tokens), BF16)})
    halves = [out[N.gram], other_core(out[N.gram])]

    def last(here, r):
        slabs = r[N.slabs].at[:rows, :slab_width]
        pairs(r[N.own], r[N.give], here, [r[N.slab]], slabs, [r[N.grads]], [0], r[N.crossed])

    out = call(
        last, place,
        {
            N.slab: far_slab, N.slabs: far_mixed_crossed, N.grads: far_grads, N.crossed: far_grads_crossed,
            N.earlier: out[N.gram],
        },
        pair_shapes(1), far=(N.earlier,),
    )
    final += [out[N.own], other_core(out[N.give])]
    return update(final, [[0], early, late, [half]], halves, factor, place, planes, slab_width)


def solution(mesh):
    spec = P(("groups", "row"), None)
    return jax.shard_map(per_device, mesh=mesh, in_specs=(spec,) * 4, out_specs=spec, check_vma=False)
```

```python
import enum

import jax
import jax.numpy as jnp
from jax import lax
from jax.experimental import pallas as pl
from jax.experimental.pallas import tpu as pltpu
from jax.sharding import PartitionSpec as P

BF16 = jnp.bfloat16
F32 = jnp.float32
MIB = 1024 * 1024
GRAM_ROWS_VMEM = 44 * MIB
UPDATE_VMEM = 22 * MIB
FETCH = True


class N(enum.Enum):
    near = enum.auto()
    rows = enum.auto()
    factor = enum.auto()
    mine = enum.auto()
    other = enum.auto()
    low = enum.auto()
    far = enum.auto()
    out = enum.auto()
    earlier = enum.auto()
    own = enum.auto()
    give = enum.auto()
    x = enum.auto()
    cross = enum.auto()
    grads = enum.auto()
    slab = enum.auto()
    chip = enum.auto()
    pair = enum.auto()
    crossed = enum.auto()
    sent = enum.auto()
    grads_crossed = enum.auto()
    slab_cross = enum.auto()
    send = enum.auto()
    products = enum.auto()
    rest = enum.auto()
    keep = enum.auto()
    sum = enum.auto()
    gram = enum.auto()
    slabs = enum.auto()


def permute(value, perm):
    return lax.ppermute(value, "row", perm)


def core_perm(n):
    return [(i, i ^ 1) for i in range(n)]


def y_perm(n):
    return [(i, i ^ 2) for i in range(n)]


def plane_perm(n, step):
    return [(i, (i + 4 * step) % n) for i in range(n)]


def call(body, place, inputs, outputs, scratch=(), limit=4 * MIB, flops=0, bytes_accessed=0, far=()):
    vmem = pl.BlockSpec(memory_space=pltpu.VMEM)
    anywhere = pl.BlockSpec(memory_space=pltpu.HBM)
    names = [*inputs, *outputs]

    def kernel(place_ref, *refs):
        body(place_ref[0], dict(zip(names, refs)), *refs[len(names):])

    results = pl.pallas_call(
        kernel,
        in_specs=[pl.BlockSpec(memory_space=pltpu.SMEM)] + [anywhere if k in far else vmem for k in inputs],
        out_specs=[vmem] * len(outputs),
        out_shape=[jax.ShapeDtypeStruct(shape, dtype) for shape, dtype in outputs.values()],
        scratch_shapes=list(scratch),
        compiler_params=pltpu.CompilerParams(vmem_limit_bytes=limit),
        cost_estimate=pl.CostEstimate(flops=flops, bytes_accessed=bytes_accessed, transcendentals=0),
    )(place, *inputs.values())
    return dict(zip(outputs, results))


def stack(out, refs):
    row = 0
    for ref in refs:
        out[row:row + ref.shape[0], :] = ref[...]
        row += ref.shape[0]


def token_blocks(groups):
    return [(k, y, core) for group in groups for core in (0, 1) for y in (0, 1) for k in group]


def shard_of(place, block, planes):
    back, other_y, other_core = block
    plane = lax.rem(place // 4 + planes - back, planes)
    y, core = lax.rem(place // 2, 2), lax.rem(place, 2)
    return plane * 4 + (1 - y if other_y else y) * 2 + (1 - core if other_core else core)


def half_block(place, planes, other):
    y = lax.rem(place // 2, 2)
    y = 1 - y if other else y
    return jnp.where(place // 4 < planes // 2, y, 1 - y)


def gram_rows(pieces, input_factor, place, planes):
    own, features = input_factor.shape
    width = features // planes
    half = planes // 2
    columns = pieces[0].shape[1]
    tokens = sum(p.shape[0] for p in pieces)
    count = len(pieces)

    def body(here, refs, sems):
        near, acc = refs[N.near], refs[N.rows]
        copies = []
        for j in range(half + 1):
            left = lax.rem(here // 4 + j, planes) * width
            size = width
            if j == half:
                size = width // 2
                left = left + half_block(here, planes, False) * size
            copies.append(
                pltpu.make_async_copy(
                    refs[N.factor].at[:, pl.ds(pl.multiple_of(left, size), size)],
                    near.at[:, j * width:j * width + size], sems.at[j],
                )
            )
            copies[-1].start()
        for j, copy in enumerate(copies):
            copy.wait()
            at = slice(j * width, min((j + 1) * width, columns))
            rows = jnp.concatenate([refs[i][:, at] for i in range(count)], 0)
            part = lax.dot_general(rows, near[:, at], (((1,), (1,)), ((), ())), preferred_element_type=F32)
            acc[...] = part * 0.5 if j == 0 else acc[...] + part

    out = call(
        body, place, {**dict(enumerate(pieces)), N.factor: input_factor},
        {N.rows: ((tokens, own), F32), N.near: ((own, columns), input_factor.dtype)},
        scratch=[pltpu.SemaphoreType.DMA((half + 1,))], limit=GRAM_ROWS_VMEM, far=(N.factor,),
        flops=2 * tokens * own * columns, bytes_accessed=2 * own * columns,
    )
    return out[N.rows], out[N.near]


def gram_part(rows, near, before, after, groups, place, planes, features, earlier):
    own, columns = near.shape
    width = features // planes
    blocks = token_blocks(groups)
    pieces = [*before, *after]
    tokens = sum(p.shape[0] for p in pieces)
    shard = tokens // len(blocks)
    count = len(pieces)
    scale = float(features) ** -0.5

    def body(here, refs, whole, total):
        ins = [refs[i] for i in range(count)]
        last = jnp.concatenate([refs[i][...] for i in range(len(before), count)], 0)
        near = refs[N.near]
        acc = 0.5 * lax.dot_general(
            last[:, :width], near[:, :width], (((1,), (1,)), ((), ())), preferred_element_type=F32
        )
        acc += lax.dot_general(last[:, width:], near[:, width:], (((1,), (1,)), ((), ())), preferred_element_type=F32)
        left = pl.multiple_of(lax.rem(here, 4) * own, own)
        at, first = 0, refs[N.rows].shape[0]
        for piece in ins:
            for low in range(0, piece.shape[0], shard):
                row = pl.multiple_of(shard_of(here, blocks[at // shard], planes) * shard, shard)
                mine = refs[N.rows][at:at + shard, :] if at < first else acc[at - first:at - first + shard, :]
                high = mine.astype(BF16)
                whole[0, pl.ds(row, shard), :] = high
                whole[1, pl.ds(row, shard), :] = (mine - high.astype(F32)).astype(BF16)
                whole[2, pl.ds(row, shard), :] = piece[low:low + shard, pl.ds(left, own)]
                at += shard
        half = lax.dot_general(whole[2], whole[0], (((1,), (1,)), ((), ())), preferred_element_type=F32)
        half += lax.dot_general(whole[2], whole[1], (((1,), (1,)), ((), ())), preferred_element_type=F32)
        total[...] = (half + half.T) * scale
        keep, give = cut(total, lax.rem(here, 2), tokens // 2)
        refs[N.mine][...] = keep
        high = give.astype(BF16)
        refs[N.other][...] = high
        refs[N.low][...] = (give - high.astype(F32)).astype(BF16)

    out = (tokens // 2, tokens)
    found = call(
        body, place,
        {**dict(enumerate(pieces)), N.rows: rows, N.near: near, **{(N.far, i): e for i, e in enumerate(earlier)}},
        {N.mine: (out, F32), N.other: (out, BF16), N.low: (out, BF16)},
        scratch=[pltpu.VMEM((3, tokens, own), BF16), pltpu.VMEM((tokens, tokens), F32)],
        limit=16 * MIB, far=[(N.far, i) for i in range(len(earlier))],
        flops=2 * tokens * own * tokens, bytes_accessed=2 * own * tokens,
    )
    return found[N.mine], found[N.other], found[N.low]


def fetch(output_factor, place, earlier):
    def body(here, refs, sem):
        copy = pltpu.make_async_copy(refs[N.factor], refs[N.out], sem)
        copy.start()
        copy.wait()

    return call(
        body, place, {N.factor: output_factor, N.earlier: earlier}, {N.out: (output_factor.shape, F32)},
        scratch=[pltpu.SemaphoreType.DMA], limit=MIB, far=(N.factor, N.earlier),
    )[N.out]


def cut(value, which, rows):
    return (
        value[pl.ds(pl.multiple_of(which * rows, rows), rows), :],
        value[pl.ds(pl.multiple_of((1 - which) * rows, rows), rows), :],
    )


def update(pieces, groups, halves, output_factor, place, planes, slab_width):
    rows, columns = output_factor.shape
    blocks = token_blocks(groups)
    tokens = sum(p.shape[0] for p in pieces)
    shard = tokens // len(blocks)
    chunk = min(1024, columns)
    scale = 1.0 / tokens
    half = tokens // 2
    count = len(pieces)

    def body(place_ref, *refs):
        ins = refs[:count]
        mine_ref, other_ref, factor_ref, out_ref, gram, grads, left_abs, left = refs[count:]
        here = place_ref[0]

        @pl.when(pl.program_id(0) == 0)
        def _():
            core = lax.rem(here, 2)
            gram[pl.ds(pl.multiple_of(core * half, half), half), :] = mine_ref[...]
            gram[pl.ds(pl.multiple_of((1 - core) * half, half), half), :] = other_ref[...]
            at = 0
            for piece in ins:
                for low in range(0, piece.shape[0], shard):
                    row = pl.multiple_of(shard_of(here, blocks[at], planes) * shard, shard)
                    grads[pl.ds(row, shard), :] = piece[low:low + shard, slab_width:]
                    at += 1
            left_abs[...] = jnp.dot(gram[...], grads[...], preferred_element_type=F32).astype(BF16)
            order = []
            for block in blocks:
                row = pl.multiple_of(shard_of(here, block, planes) * shard, shard)
                order.append(left_abs[pl.ds(row, shard), :])
            left[...] = jnp.concatenate(order, 0).T

        at = pl.ds(pl.multiple_of(pl.program_id(0) * chunk, chunk), chunk)
        part = jnp.concatenate([p[:, at] for p in ins], 0)
        base = factor_ref[:, at] if FETCH else factor_ref[...]
        out_ref[...] = base + jnp.dot(left[...], part, preferred_element_type=F32) * scale

    vmem = pl.BlockSpec(memory_space=pltpu.VMEM)
    return pl.pallas_call(
        body,
        grid=(columns // chunk,),
        in_specs=[pl.BlockSpec(memory_space=pltpu.SMEM)] + [vmem] * (count + 2)
        + [vmem if FETCH else pl.BlockSpec((rows, chunk), lambda j: (0, j))],
        out_specs=pl.BlockSpec((rows, chunk), lambda j: (0, j)),
        scratch_shapes=[
            pltpu.VMEM((tokens, tokens), BF16), pltpu.VMEM((tokens, rows), BF16), pltpu.VMEM((tokens, rows), BF16),
            pltpu.VMEM((rows, tokens), BF16),
        ],
        out_shape=jax.ShapeDtypeStruct((rows, columns), F32),
        compiler_params=pltpu.CompilerParams(vmem_limit_bytes=UPDATE_VMEM),
        cost_estimate=pl.CostEstimate(
            flops=2 * rows * tokens * (columns + tokens), bytes_accessed=8 * rows * columns, transcendentals=0
        ),
    )(place, *pieces, *halves, output_factor)


def per_device(inputs, input_factor, out_grads, output_factor):
    n = lax.axis_size("row")
    planes = n // 4
    half = planes // 2
    place = lax.axis_index("row").reshape(1)
    near = sorted((k for k in range(1, planes) if k != half), key=lambda k: (k != half - 1, min(k, planes - k)))
    early, late = near[: len(near) // 2], near[len(near) // 2:]
    rows, features = inputs.shape
    width, used = features // planes, half + 1
    x_width = half * width + width // 2
    slab_width = output_factor.shape[1]
    own_width = out_grads.shape[1] // n
    cross_width = slab_width + 2 * own_width
    pair_width = slab_width + own_width
    x_shape = ((rows, x_width), BF16)

    def across(value):
        return permute(value, y_perm(n))

    def other_core(value):
        return permute(value, core_perm(n))

    def ahead(value, k):
        return permute(value, plane_perm(n, k))

    def y_of(here):
        return lax.rem(here // 2, 2)

    def columns(ref, first, count, size):
        return ref[:, pl.ds(pl.multiple_of(first * size, size), count * size)]

    def take(out, row, ref, here, other):
        size = width // 2
        out[row:row + rows, : half * width] = ref[:, : half * width]
        left = pl.multiple_of(half * width + half_block(here, planes, other) * size, size)
        out[row:row + rows, half * width:] = ref[:, pl.ds(left, size)]

    def grads_ahead(grads, here, k):
        return columns(grads, lax.rem(here // 4 + k, planes), 1, 4 * own_width)

    def for_neighbour(ref, here, low=0):
        return ref[:, pl.ds(pl.multiple_of(low + (1 - y_of(here)) * 2 * own_width, own_width), 2 * own_width)]

    def pair(own, give, row, slab, grads, here):
        core = lax.rem(here, 2)
        for out, c in ((own, core), (give, 1 - core)):
            out[row:row + rows, :slab_width] = slab
            out[row:row + rows, slab_width:] = grads(c)

    def pairs(own, give, here, slabs, slabs_crossed, grads, lows, grads_crossed):
        y = y_of(here)
        for i, ref in enumerate(slabs):
            mine = lambda c, i=i: grads[i][
                :, pl.ds(pl.multiple_of(lows[i] + (y * 2 + c) * own_width, own_width), own_width)
            ]
            pair(own, give, i * rows, ref[:, :slab_width], mine, here)
        for i in range(len(slabs)):
            at = slice(i * rows, (i + 1) * rows)
            mine = lambda c, at=at: grads_crossed[at, pl.ds(pl.multiple_of(c * own_width, own_width), own_width)]
            pair(own, give, (len(slabs) + i) * rows, slabs_crossed[at, :], mine, here)

    def pair_shapes(count):
        return {k: ((2 * count * rows, pair_width), BF16) for k in (N.own, N.give)}

    slab_shape, grads_shape = ((rows, slab_width), BF16), ((rows, 4 * own_width), BF16)
    wide_shape = ((rows, slab_width + 4 * own_width), BF16)
    together = half - 1 == 1

    blocks = {k: used + (k == half - 1) for k in near}

    def first(here, r):
        plane = here // 4
        for k in near:
            for j in range(blocks[k]):
                r[k][:, j * width:(j + 1) * width] = columns(r[N.x], lax.rem(plane + k + j, planes), 1, width)
        for name, other in ((N.own, False), (N.cross, True)):
            for j in range(half):
                r[name][:, j * width:(j + 1) * width] = columns(r[N.x], lax.rem(plane + j, planes), 1, width)
            at = lax.rem(plane + half, planes) * 2 + half_block(here, planes, other)
            r[name][:, half * width:] = columns(r[N.x], at, 1, width // 2)

    def first_grads(here, r):
        plane = here // 4
        r[N.cross][:, :slab_width] = r[N.grads][:, :slab_width]
        r[N.cross][:, slab_width:] = columns(r[N.grads], plane * 2 + 1 - y_of(here), 1, 2 * own_width)
        r[N.slab][...] = r[N.grads][:, :slab_width]
        r[N.chip][...] = columns(r[N.grads], plane * 2 + y_of(here), 1, 2 * own_width)
        for k in range(1, planes):
            r[k][...] = grads_ahead(r[N.grads], here, k)

    out = call(
        first, place, {N.x: inputs},
        {**{k: ((rows, blocks[k] * width), BF16) for k in near}, N.own: x_shape, N.cross: x_shape},
    )
    own = out[N.own]
    got = {k: ahead(out[k], k) for k in near}
    crossed_0 = across(out[N.cross])
    sent = call(
        first_grads, place, {N.grads: out_grads},
        {
            N.cross: ((rows, cross_width), BF16), N.slab: slab_shape, N.chip: ((rows, 2 * own_width), BF16),
            **{k: grads_shape for k in range(1, planes)},
        },
    )
    grads_crossed_0 = across(sent[N.cross])

    def second(here, r):
        r[N.far][...] = r[half - 1][:, width:]
        for i, k in enumerate(near):
            take(r[N.near], i * rows, r[k], here, True)
        stack(r[N.pair], [r[N.own], r[N.crossed]])
        r[N.slab][...] = r[N.sent][...]

    out = call(
        second, place,
        {
            **{k: got[k] for k in near}, N.own: own, N.crossed: crossed_0, N.sent: sent[N.slab],
            N.grads_crossed: grads_crossed_0,
        },
        {
            N.far: ((rows, used * width), BF16), N.near: ((len(near) * rows, x_width), BF16),
            N.pair: ((2 * rows, x_width), BF16), N.slab: slab_shape,
        },
        far=(N.grads_crossed,),
    )
    pair_0 = out[N.pair]
    far = ahead(out[N.far], 1)
    crossed_near = across(out[N.near])
    pair_0_other = other_core(pair_0)
    slab_got = {k: ahead(out[N.slab], k) for k in early}

    def third(here, r):
        take(r[N.cross], 0, r[N.far], here, True)
        for i, k in enumerate(near):
            take(r[N.pair], i * rows, r[k], here, False)
        r[N.pair][len(near) * rows:, :] = r[N.crossed][...]
        stack(r[N.slab_cross], [r[N.slab, k] for k in early])
        for k in early:
            if together and k == half - 1:
                r[N.send, k][:, :slab_width] = r[N.slab, k][...]
                r[N.send, k][:, slab_width:] = r[N.sent, k][...]
            else:
                r[N.send, k][...] = r[N.sent, k][...]
        if not together:
            r[N.slab][...] = r[N.slab, half - 1][...]

    out = call(
        third, place,
        {
            **{k: got[k] for k in near}, N.far: far, N.crossed: crossed_near, N.other: pair_0_other,
            **{(N.sent, k): sent[k] for k in early}, **{(N.slab, k): slab_got[k] for k in early},
        },
        {
            N.cross: x_shape, N.pair: ((2 * len(near) * rows, x_width), BF16),
            N.slab_cross: ((len(early) * rows, slab_width), BF16), **({} if together else {N.slab: slab_shape}),
            **{(N.send, k): wide_shape if together and k == half - 1 else grads_shape for k in early},
        },
    )
    pair_near = out[N.pair]
    crossed_far = across(out[N.cross])
    pair_near_other = other_core(pair_near)
    grads_got = {k: (ahead(out[N.send, k], k), slab_width if together and k == half - 1 else 0) for k in early}
    far_slab = grads_got[half - 1][0] if together else ahead(out[N.slab], 1)
    slab_early_crossed = across(out[N.slab_cross])
    before = [pair_0, pair_0_other, pair_near, pair_near_other]
    products, blocks_here = gram_rows(before, input_factor, place, planes)

    def fourth(here, r):
        take(r[N.pair], 0, r[N.far], here, False)
        r[N.pair][rows:, :] = r[N.crossed][...]
        r[N.send][...] = r[N.sent, half][...]
        for k in late:
            r[N.send, k][:, :slab_width] = r[N.sent][...]
            r[N.send, k][:, slab_width:] = r[N.sent, k][...]

    out = call(
        fourth, place,
        {
            N.far: far, N.crossed: crossed_far, N.other: pair_near_other, N.products: products,
            N.sent: sent[N.slab], **{(N.sent, k): sent[k] for k in [*late, half]},
            **{(N.grads, k): grads_got[k][0] for k in early}, N.slab_cross: slab_early_crossed,
        },
        {N.pair: ((2 * rows, x_width), BF16), N.send: grads_shape, **{(N.send, k): wide_shape for k in late}},
        far=(N.products, N.slab_cross, *[(N.grads, k) for k in early]),
    )
    after = [out[N.pair], other_core(out[N.pair])]
    for k in late:
        slab_got[k] = ahead(out[N.send, k], k)
        grads_got[k] = (slab_got[k], slab_width)
    far_grads = ahead(out[N.send], half)

    def own_pair(here, r):
        mine = lambda c: columns(r[N.chip], c, 1, own_width)
        pair(r[N.own], r[N.give], 0, r[N.slab][...], mine, here)
        mine = lambda c: r[N.crossed][:, pl.ds(pl.multiple_of(slab_width + c * own_width, 128), own_width)]
        pair(r[N.own], r[N.give], rows, r[N.crossed][:, :slab_width], mine, here)

    out = call(
        own_pair, place, {N.slab: sent[N.slab], N.chip: sent[N.chip], N.crossed: grads_crossed_0}, pair_shapes(1)
    )
    final = [out[N.own], other_core(out[N.give])]
    mine, other, rest = gram_part(products, blocks_here, before, after, [[0], near, [half]], place, planes, features, [])
    tokens = mine.shape[1]
    other, rest = other_core(other), other_core(rest)

    quarter = tokens // 4

    def fifth(here, r, total):
        total[...] = r[N.mine][...] + (r[N.other][...].astype(F32) + r[N.rest][...].astype(F32))
        keep, give = cut(total, y_of(here), quarter)
        r[N.keep][...] = keep
        r[N.low][...] = give.astype(BF16)

    out = call(
        fifth, place, {N.mine: mine, N.other: other, N.rest: rest},
        {N.keep: ((quarter, tokens), F32), N.low: ((quarter, tokens), BF16)},
        scratch=[pltpu.VMEM((2 * quarter, tokens), F32)],
    )
    total, low = out[N.keep], across(out[N.low])

    def late_across(here, r):
        for i, k in enumerate(late):
            at = slice(i * rows, (i + 1) * rows)
            r[N.cross][at, :slab_width] = r[N.grads, k][:, :slab_width]
            r[N.cross][at, slab_width:] = for_neighbour(r[N.grads, k], here, grads_got[k][1])

    mixed_shape = ((len(late) * rows, cross_width), BF16)
    late_out = call(
        late_across, place,
        {N.earlier: out[N.low], **{(N.grads, k): grads_got[k][0] for k in late}},
        {N.cross: mixed_shape}, far=(N.earlier,),
    )
    mixed_crossed = across(late_out[N.cross])

    def add(here, r):
        total = r[N.mine][...] + r[N.other][...].astype(F32)
        r[N.sum][...] = total
        r[N.low][...] = total.astype(BF16)

    def add_near(here, r):
        add(here, r)
        for i, k in enumerate(early):
            at = slice(i * rows, (i + 1) * rows)
            r[N.cross][at, slab_width:] = for_neighbour(r[N.grads, k], here, grads_got[k][1])
        r[N.cross][:rows, :slab_width] = r[N.slab][:, :slab_width]

    shapes = {N.sum: (total.shape, F32), N.low: (total.shape, BF16)}
    out = call(
        add_near, place,
        {
            N.mine: total, N.other: low, N.slab: far_slab, N.earlier: late_out[N.cross],
            **{(N.grads, k): grads_got[k][0] for k in early},
        },
        {**shapes, N.cross: mixed_shape}, far=(N.earlier,),
    )
    far_mixed_crossed = across(out[N.cross])
    factor = fetch(output_factor, place, out[N.sum])
    def far_grads_across(here, r):
        r[N.cross][...] = for_neighbour(r[N.grads], here)

    step = 4
    while step < n:
        low = permute(out[N.low], [(i, i ^ step) for i in range(n)])
        ins = {N.mine: out[N.sum], N.other: low}
        if step == 4:
            ins.update({N.factor: factor, N.crossed: far_mixed_crossed, N.grads: far_grads})
            out = call(add, place, ins, shapes, far=(N.factor, N.crossed, N.grads))
            first_sum = out[N.sum]
        else:
            out = call(add, place, {**ins, N.crossed: mixed_crossed}, shapes, far=(N.crossed,))
        step *= 2
    summed = out[N.sum]
    far_sent = call(
        far_grads_across, place, {N.grads: far_grads, N.earlier: first_sum},
        {N.cross: ((rows, 2 * own_width), BF16)}, far=(N.earlier,),
    )
    far_grads_crossed = across(far_sent[N.cross])

    def near_pairs(here, r):
        mixed, far_mixed = r[N.crossed], r[N.far]
        sources = (
            (early, r[N.slab], far_mixed.at[:, slab_width:]),
            (late, mixed.at[:, :slab_width], mixed.at[:, slab_width:]),
        )
        for i, (some, slabs, crossed) in enumerate(sources):
            own_slabs = [r[N.slab, k] if k in early else r[N.grads, k] for k in some]
            grads = [r[N.grads, k] for k in some]
            pairs(r[N.own, i], r[N.give, i], here, own_slabs, slabs, grads, [grads_got[k][1] for k in some], crossed)

    pair_out = call(
        near_pairs, place,
        {
            N.slab: slab_early_crossed, N.crossed: mixed_crossed, N.far: far_mixed_crossed, N.earlier: summed,
            **{(N.slab, k): slab_got[k] for k in early}, **{(N.grads, k): grads_got[k][0] for k in near},
        },
        {(k, i): shape for i, some in enumerate((early, late)) for k, shape in pair_shapes(len(some)).items()},
        far=(N.earlier,),
    )
    for i in range(2):
        final += [pair_out[N.own, i], other_core(pair_out[N.give, i])]

    low = out[N.low]

    def join(here, r):
        y = y_of(here)
        r[N.gram][pl.ds(pl.multiple_of(y * quarter, quarter), quarter), :] = r[N.mine][...]
        r[N.gram][pl.ds(pl.multiple_of((1 - y) * quarter, quarter), quarter), :] = r[N.other][...]

    out = call(join, place, {N.mine: low, N.other: across(low)}, {N.gram: ((2 * quarter, tokens), BF16)})
    halves = [out[N.gram], other_core(out[N.gram])]

    def last(here, r):
        slabs = r[N.slabs].at[:rows, :slab_width]
        pairs(r[N.own], r[N.give], here, [r[N.slab]], slabs, [r[N.grads]], [0], r[N.crossed])

    out = call(
        last, place,
        {
            N.slab: far_slab, N.slabs: far_mixed_crossed, N.grads: far_grads, N.crossed: far_grads_crossed,
            N.earlier: summed,
        },
        pair_shapes(1), far=(N.earlier,),
    )
    final += [out[N.own], other_core(out[N.give])]
    return update(final, [[0], early, late, [half]], halves, factor, place, planes, slab_width)


def solution(mesh):
    spec = P(("groups", "row"), None)
    return jax.shard_map(per_device, mesh=mesh, in_specs=(spec,) * 4, out_specs=spec, check_vma=False)
```
